32 devices in a mesh: groups: 2 (over y), space: 4 (over z), depth: 4 (over x, core).
Axes of the slice: x: 2, y: 2, z: 4, core: 2. Of those that a mesh axis runs over, the one named last changes fastest.
Arguments:
- features: bfloat16 [128, 32, 64, 128], P(('groups', 'space'), None, 'depth'), parts along dimension 0, may hold values from -6 to 6
- occupancy: int32 [16, 8, 16], P(('groups', 'space'), 'depth'), parts along dimension 0, may hold values 0 or 1
- weight_one: bfloat16 [32, 864], replicated, may hold values from -0.21875 to 0.21875
- weight_two: bfloat16 [32, 864], replicated, may hold values from -0.21875 to 0.21875
- cotangent: bfloat16 [128, 32, 64, 128], P(('groups', 'space'), None, 'depth'), parts along dimension 0, may hold values from -6 to 6
Outputs:
- output: bfloat16 [128, 32, 64, 128], P(('groups', 'space'), None, 'depth'), parts along dimension 0
- grad_input: bfloat16 [128, 32, 64, 128], P(('groups', 'space'), None, 'depth'), parts along dimension 0
- grad_one: float32 [64, 864], P('groups'), parts along dimension 0
- grad_two: float32 [64, 864], P('groups'), parts along dimension 0
The draws below stay inside these ranges and needn't reach their ends.
There are 2 independent parts, one for each index of `groups`. The reference program is written for one: setup_inputs(seed, part) draws one part's arguments, and reference() takes and returns one part's arrays. A program takes and returns all parts, laid end to end along the dimension named above; an argument that names none is the same for every part. Nothing has to cross between parts.
All inputs are finite; a program needn't handle non-finite values. No bound on the sum of `occupancy` on one device may be relied on, other than what follows from the above.
Results may differ from the reference program's by a relative error of at most 0.0051.
Values may be sent and summed in bfloat16 or wider, within the bound.
No kernel may reach another device: no remote copies, remote signals or barrier semaphores. Data moves between devices by JAX's collectives and lax.ppermute only.
A program may use at most 512 MiB of HBM per device.

```python
import jax
import jax.numpy as jnp
from jax import lax

C = 32
BRICK = 8
NZ = 128
NX = 64
NY = 64


def touch_ends(drawn, rng, smallest, top_value):
    longest = drawn.shape.index(max(drawn.shape))
    spots = []
    for shift in (0, 1):
        where = [jax.random.randint(jax.random.fold_in(rng, axis), (), 0, length) for axis, length in enumerate(drawn.shape)]
        where[longest] = (where[longest] + shift) % drawn.shape[longest]
        spots.append(tuple(where))
    return drawn.at[spots[0]].set(smallest).at[spots[1]].set(top_value)


def block_levels(key, shape, pieces, least, largest):
    def one(dim, shards_of):
        draws = jax.random.uniform(jax.random.fold_in(jax.random.fold_in(key, 6), dim), (shards_of,), jnp.float32, least / len(pieces), largest / len(pieces))
        return jnp.repeat(jnp.exp(draws), shape[dim] // shards_of).reshape((-1,) + (1,) * (len(shape) - dim - 1))

    loudness = one(*pieces[0])
    for cut in pieces[1:]:
        loudness = loudness * one(*cut)
    return loudness


def noise(stream_key, dims, spread, bound, split=(), kind=jnp.bfloat16):
    gain = block_levels(stream_key, dims, split, -0.22, 0.18) if split else 1.0
    values = jax.random.normal(stream_key, dims, jnp.float32) * spread * gain
    return jnp.minimum(jnp.maximum(values, -bound), bound).astype(kind)


def setup_inputs(seed: int = 0, part: int = 0) -> dict:
    arg_keys = jax.random.split(jax.random.key(seed), 6)
    part_splits = jax.random.split(jax.random.fold_in(arg_keys[5], part), 6)
    return {
        "features": noise(part_splits[0], (NX, C, NY, NZ), 1.0, 6.0, ((0, 4), (2, 4))),
        "occupancy": touch_ends((jax.random.randint(part_splits[1], (NX // BRICK, NY // BRICK, NZ // BRICK), 0, 5) < 3).astype(jnp.int32), jax.random.fold_in(part_splits[1], 1), 0, 1),
        "weight_one": noise(arg_keys[2], (C, 27 * C), (27 * C) ** -0.5, 0.21875),
        "weight_two": noise(arg_keys[3], (C, 27 * C), (27 * C) ** -0.5, 0.21875),
        "cotangent": noise(part_splits[4], (NX, C, NY, NZ), 1.0, 6.0, ((0, 4), (2, 4))),
    }


def expand(occupancy):
    grid = jnp.repeat(occupancy, BRICK, axis=0)
    grid = jnp.repeat(grid, BRICK, axis=1)
    return jnp.repeat(grid, BRICK, axis=2)

def flipped(weight):
    width = weight.shape[0]
    return weight.reshape(width, 27, width)[:, ::-1, :].transpose(2, 1, 0).reshape(width, 27 * width)

def apply_kernel(weight, field):
    width = weight.shape[0]
    kernel = weight.reshape(width, 3, 3, 3, width).astype(jnp.float32)
    result = lax.conv_general_dilated(field.astype(jnp.float32)[None], kernel, (1, 1, 1), ((1, 1), (1, 1), (1, 1)), dimension_numbers=('NDCHW', 'ODHWI', 'NDCHW'), precision=lax.Precision.HIGHEST)
    return result[0]

def kernel_grad(grad, field):
    size_x, width, size_y, size_z = field.shape
    padded = jnp.pad(field.astype(jnp.float32), ((1, 1), (0, 0), (1, 1), (1, 1)))
    grad_wide = grad.astype(jnp.float32)
    terms = []
    for step_x in range(3):
        for step_y in range(3):
            for step_z in range(3):
                window = padded[step_x:step_x + size_x, :, step_y:step_y + size_y, step_z:step_z + size_z]
                terms.append(jnp.einsum('xcyz,xdyz->cd', grad_wide, window, precision=lax.Precision.HIGHEST))
    return jnp.stack(terms, axis=1).reshape(width, 27 * width)

def reference(features, occupancy, weight_one, weight_two, cotangent):
    mask = expand(occupancy)[:, None].astype(jnp.bfloat16)
    inputs = features * mask
    pre_act = apply_kernel(weight_one, inputs)
    hidden = (jax.nn.silu(pre_act) * mask).astype(jnp.bfloat16)
    output = (apply_kernel(weight_two, hidden) * mask).astype(jnp.bfloat16)
    out_grad = cotangent * mask
    hid_grad = apply_kernel(flipped(weight_two), out_grad)
    sig = jax.nn.sigmoid(pre_act)
    pre_grad = (hid_grad * sig * (1.0 + pre_act * (1.0 - sig)) * mask).astype(jnp.bfloat16)
    grad_input = (apply_kernel(flipped(weight_one), pre_grad) * mask).astype(jnp.bfloat16)
    grad_one = kernel_grad(pre_grad, inputs) / NX
    grad_two = kernel_grad(out_grad, hidden) / NX
    return (output, grad_input, grad_one, grad_two)
```

```python
import functools

import jax
import jax.numpy as jnp
from jax import lax
from jax.experimental import pallas as pl
from jax.experimental.pallas import tpu as pltpu
from jax.sharding import PartitionSpec as P

BRICK = 8
BX, BY = 2, 4
IX, IY = BX + 2, BY + 2
BF = jnp.bfloat16
F32 = jnp.float32
VMEM = pltpu.VMEM
ANY = pl.ANY
LIMIT = 56 << 20


def cost(us):
    return pl.CostEstimate(flops=int(us * 1.1e9), bytes_accessed=1 << 20, transcendentals=0)


def lane_ids(shape):
    return lax.broadcasted_iota(jnp.int32, shape, len(shape) - 1)


def relayout_kernel(par, mask, feat, cot, a_in, a_og, rim_a, rim_b, scratch):
    step = pl.program_id(0)
    rows = feat.shape[0]
    width, size_y = feat.shape[1], feat.shape[2]
    odd = par[1]
    for which, (src, dst) in enumerate(((feat, a_in), (cot, a_og))):
        for r in range(rows):
            scratch[which, r] = src[r].reshape(width * size_y, 128).astype(F32)
    for which, dst in enumerate((a_in, a_og)):
        for r in range(rows):
            brick_x = (step * rows + r) // BRICK
            for y in range(size_y):
                m = mask[brick_x, y // BRICK]
                value = scratch[which, r, pl.ds(y, width, stride=size_y), :]
                dst[r, y] = (value * m).astype(BF)

    for which, src in enumerate((a_in, a_og)):
        put_rims(odd, which, src, rim_a, rim_b)


def put_rims(odd, which, src, rim_a, rim_b):
    size_y = src.shape[1]

    @pl.when(odd == 1)
    def _():
        rim_a[which] = src[:, 0]
        rim_b[which] = src[:, size_y - 1]

    @pl.when(odd == 0)
    def _():
        rim_a[which] = src[:, size_y - 1]
        rim_b[which] = src[:, 0]


def relayout(par, mask, feat, cot):
    size_x, width, size_y, size_z = feat.shape
    rows = 4
    native = pl.BlockSpec((rows, width, size_y, size_z), lambda i: (i, 0, 0, 0))
    ours = pl.BlockSpec((rows, size_y, width, size_z), lambda i: (i, 0, 0, 0))
    rim = pl.BlockSpec((2, rows, width, size_z), lambda i: (0, i, 0, 0))
    arr = jax.ShapeDtypeStruct((size_x, size_y, width, size_z), BF)
    rim_shape = jax.ShapeDtypeStruct((2, size_x, width, size_z), BF)
    return pl.pallas_call(
        relayout_kernel,
        grid=(size_x // rows,),
        in_specs=[
            pl.BlockSpec(memory_space=pltpu.SMEM),
            pl.BlockSpec(memory_space=VMEM),
            native,
            native,
        ],
        out_specs=[ours, ours, rim, rim],
        out_shape=[arr, arr, rim_shape, rim_shape],
        scratch_shapes=[VMEM((2, rows, width * size_y, size_z), F32)],
        compiler_params=pltpu.CompilerParams(vmem_limit_bytes=LIMIT),
        cost_estimate=cost(6),
        name="relayout",
    )(par, mask, feat, cot)


def bands_kernel(w_ref, *outs):
    width = 32
    lanes = lane_ids((width, 128))

    def band(pick, out):
        base = [[jnp.zeros((width, 128), F32) for _ in range(6)] for _ in range(3)]
        for dx in range(3):
            for dy in range(3):
                for dz in range(3):
                    at = (dx * IY + dy) * width
                    piece, lane = pick((dx * 3 + dy) * 3 + dz)
                    shift = (at - lane) % 128
                    if shift:
                        piece = pltpu.roll(piece, shift, 1)
                    here = (lanes // width) == (at % 128) // width
                    base[dz][at // 128] = jnp.where(here, piece, base[dz][at // 128])
        zero = jnp.zeros((width, 128), F32)
        for dz in range(3):
            turned = {0: base[dz]}
            for q in range(1, 4):
                rolled = [pltpu.roll(b, q * width, 1) for b in base[dz]]
                turned[q] = [
                    jnp.where(lanes < q * width, rolled[k - 1] if k else zero, rolled[k])
                    for k in range(6)
                ]
            for xo in range(BX):
                for yo in range(BY):
                    off = xo * IY + yo
                    whole, part = off // 4, off % 4
                    row = ((dz * BX + xo) * BY + yo) * width
                    for k in range(6):
                        src = turned[part][k - whole] if k >= whole else zero
                        out[row : row + width, k * 128 : (k + 1) * 128] = src.astype(BF)

    def straight(which):
        def pick(tap):
            lane = tap * width
            col = lane // 128 * 128
            return w_ref[which, :, col : col + 128], lane % 128

        return pick

    def flipped(which):
        pad = jnp.zeros((128 - width, 896), F32)
        turned = jnp.concatenate([w_ref[which], pad], 0).T

        def pick(tap):
            back = 26 - tap
            return turned[back * width : (back + 1) * width], 0

        return pick

    band(straight(0), outs[0])
    band(flipped(1), outs[1])
    band(straight(1), outs[2])
    band(flipped(0), outs[3])


def bands(weight_one, weight_two):
    w = jnp.stack([weight_one, weight_two]).astype(F32)
    w = jnp.pad(w, ((0, 0), (0, 0), (0, 896 - w.shape[2])))
    shape = jax.ShapeDtypeStruct((3 * BX * BY * 32, IX * IY * 32), BF)
    return pl.pallas_call(
        bands_kernel,
        in_specs=[pl.BlockSpec(memory_space=VMEM)],
        out_specs=[pl.BlockSpec(memory_space=VMEM)] * 4,
        out_shape=[shape] * 4,
        compiler_params=pltpu.CompilerParams(vmem_limit_bytes=LIMIT),
        cost_estimate=cost(4),
        name="bands",
    )(w)


def fill(par, arrays, rim_d, rim_s, padded, sem, which_of=(0, 1)):
    odd_s, odd_d = par[0], par[1]
    size_x, size_y = arrays[0].shape[0], arrays[0].shape[1]
    spot_da = jnp.where(odd_d == 1, 0, size_y + 1)
    spot_db = size_y + 1 - spot_da
    spot_sa = jnp.where(odd_s == 1, 0, size_x + 1)
    spot_sb = size_x + 1 - spot_sa
    copies = []
    for slot, (arr, which) in enumerate(zip(arrays, which_of)):
        copies += [
            (arr, padded.at[slot, pl.ds(1, size_x), pl.ds(1, size_y)]),
            (rim_d[0].at[which], padded.at[slot, pl.ds(1, size_x), spot_da]),
            (rim_d[1].at[which], padded.at[slot, pl.ds(1, size_x), spot_db]),
            (rim_s[0].at[which], padded.at[slot, spot_sa]),
            (rim_s[1].at[which], padded.at[slot, spot_sb]),
        ]
    made = [pltpu.make_async_copy(s, d, sem.at[i]) for i, (s, d) in enumerate(copies)]
    for c in made:
        c.start()
    return made


def block_input(padded, slot, bx, pair):
    parts = []
    for by in (2 * pair, 2 * pair + 1):
        part = padded[slot, pl.ds(BX * bx, IX), BY * by : BY * by + IY]
        parts.append(part.reshape(IX * IY * 32, 128))
    return jnp.concatenate(parts, 1)


def z_sum(product, half):
    n = BX * BY * 32
    p = product[:, half * 128 : (half + 1) * 128]
    lanes = lane_ids((n, 128))
    below = jnp.where(lanes > 0, pltpu.roll(p[:n], 1, 1), 0.0)
    above = jnp.where(lanes < 127, pltpu.roll(p[2 * n :], 127, 1), 0.0)
    return p[n : 2 * n] + below + above


def first_kernel(
    par, mask, t_one, t_two, a_in, a_og, da, db, sa, sb, hid, pre, rim_a, rim_b, padded, sem
):
    bx = pl.program_id(0)

    @pl.when(bx == 0)
    def _():
        for c in fill(par, (a_in, a_og), (da, db), (sa, sb), padded, sem):
            c.wait()

    for pair in range(hid.shape[1] // (2 * BY)):
        one = jnp.dot(t_one[...], block_input(padded, 0, bx, pair), preferred_element_type=F32)
        two = jnp.dot(t_two[...], block_input(padded, 1, bx, pair), preferred_element_type=F32)
        for half in range(2):
            by = 2 * pair + half
            m = mask[bx * BX // BRICK, by * BY // BRICK]
            act = z_sum(one, half)
            grad = z_sum(two, half)
            sig = 1.0 / (1.0 + jnp.exp(-act))
            hidden = (act * sig * m).astype(BF)
            slope = (grad * sig * (1.0 + act * (1.0 - sig)) * m).astype(BF)
            hid[:, by * BY : (by + 1) * BY] = hidden.reshape(BX, BY, 32, 128)
            pre[:, by * BY : (by + 1) * BY] = slope.reshape(BX, BY, 32, 128)
    put_rims(par[1], 0, hid, rim_a, rim_b)
    put_rims(par[1], 1, pre, rim_a, rim_b)


SM = pl.BlockSpec(memory_space=pltpu.SMEM)
VM = pl.BlockSpec(memory_space=VMEM)
HB = pl.BlockSpec(memory_space=ANY)


def padded_scratch(n, arr):
    size_x, size_y, width, size_z = arr.shape
    return VMEM((n, size_x + 2, size_y + 2, width, size_z), BF)


def first(par, mask, t_one, t_two, a_in, a_og, da, db, sa, sb):
    size_x, size_y, width, size_z = a_in.shape
    ours = pl.BlockSpec((BX, size_y, width, size_z), lambda i: (i, 0, 0, 0))
    rim = pl.BlockSpec((2, BX, width, size_z), lambda i: (0, i, 0, 0))
    arr = jax.ShapeDtypeStruct(a_in.shape, BF)
    rim_shape = jax.ShapeDtypeStruct(da.shape, BF)
    return pl.pallas_call(
        first_kernel,
        grid=(size_x // BX,),
        in_specs=[SM, VM, VM, VM] + [HB] * 6,
        out_specs=[ours, ours, rim, rim],
        out_shape=[arr, arr, rim_shape, rim_shape],
        scratch_shapes=[padded_scratch(2, a_in), pltpu.SemaphoreType.DMA((10,))],
        compiler_params=pltpu.CompilerParams(vmem_limit_bytes=LIMIT),
        cost_estimate=cost(18),
        name="first",
    )(par, mask, t_one, t_two, a_in, a_og, da, db, sa, sb)


def second_kernel(par, mask, t, arr, da, db, sa, sb, out, padded, scratch, sem, *, which):
    bx = pl.program_id(0)
    width, size_y = out.shape[1], out.shape[2]

    @pl.when(bx == 0)
    def _():
        for c in fill(par, (arr,), (da, db), (sa, sb), padded, sem, (which,)):
            c.wait()

    for pair in range(size_y // (2 * BY)):
        product = jnp.dot(t[...], block_input(padded, 0, bx, pair), preferred_element_type=F32)
        for half in range(2):
            by = 2 * pair + half
            m = mask[bx * BX // BRICK, by * BY // BRICK]
            value = z_sum(product, half) * m
            for xo in range(BX):
                for yo in range(BY):
                    row = (xo * BY + yo) * 32
                    y = by * BY + yo
                    scratch[xo, pl.ds(y, width, stride=size_y), :] = value[row : row + 32]
    for xo in range(BX):
        out[xo] = scratch[xo].astype(BF).reshape(width, size_y, 128)


def second(par, mask, t, arr, da, db, sa, sb, which):
    size_x, size_y, width, size_z = arr.shape
    native = pl.BlockSpec((BX, width, size_y, size_z), lambda i: (i, 0, 0, 0))
    return pl.pallas_call(
        functools.partial(second_kernel, which=which),
        grid=(size_x // BX,),
        in_specs=[SM, VM, VM] + [HB] * 5,
        out_specs=native,
        out_shape=jax.ShapeDtypeStruct((size_x, width, size_y, size_z), BF),
        scratch_shapes=[
            padded_scratch(1, arr),
            VMEM((BX, width * size_y, size_z), F32),
            pltpu.SemaphoreType.DMA((5,)),
        ],
        compiler_params=pltpu.CompilerParams(vmem_limit_bytes=LIMIT),
        cost_estimate=cost(12),
        name="second",
    )(par, mask, t, arr, da, db, sa, sb)


def grad_kernel(par, g, arr, da, db, sa, sb, out, padded, total, sem, *, which):
    bx = pl.program_id(0)
    size_y = g.shape[1]
    n = BX * BY * 32

    @pl.when(bx == 0)
    def _():
        for c in fill(par, (arr,), (da, db), (sa, sb), padded, sem, (which,)):
            c.wait()
        total[...] = jnp.zeros_like(total)

    rows = []
    for by in range(size_y // BY):
        block = g[:, by * BY : (by + 1) * BY].reshape(n, 128).astype(F32)
        lanes = lane_ids((n, 128))
        ahead = jnp.where(lanes < 127, pltpu.roll(block, 127, 1), 0.0)
        behind = jnp.where(lanes > 0, pltpu.roll(block, 1, 1), 0.0)
        rows.append(jnp.concatenate([ahead, block, behind], 0).astype(BF))
    lhs = jnp.concatenate(rows, 1)
    rhs = jnp.concatenate([block_input(padded, 0, bx, p) for p in range(size_y // (2 * BY))], 1)
    total[...] += lax.dot_general(lhs, rhs, (((1,), (1,)), ((), ())), preferred_element_type=F32)

    @pl.when(bx == pl.num_programs(0) - 1)
    def _():
        lanes = IX * IY * 32
        for dz in range(3):
            acc = jnp.zeros((32, lanes), F32)
            for xo in range(BX):
                for yo in range(BY):
                    row = ((dz * BX + xo) * BY + yo) * 32
                    part = total[row : row + 32, :]
                    shift = (xo * IY + yo) * 32
                    acc += pltpu.roll(part, lanes - shift, 1) if shift else part
            for dx in range(3):
                at = dx * IY * 32
                moved = pltpu.roll(acc, lanes - at, 1) if at else acc
                out[dx, dz * 32 : (dz + 1) * 32, :] = moved[:, :128]


def kernel_grad(par, g, arr, da, db, sa, sb, which):
    size_x, size_y, width, size_z = arr.shape
    ours = pl.BlockSpec((BX, size_y, width, size_z), lambda i: (i, 0, 0, 0))
    return pl.pallas_call(
        functools.partial(grad_kernel, which=which),
        grid=(size_x // BX,),
        in_specs=[SM, ours] + [HB] * 5,
        out_specs=VM,
        out_shape=jax.ShapeDtypeStruct((3, 96, 128), F32),
        scratch_shapes=[
            padded_scratch(1, arr),
            VMEM((3 * BX * BY * 32, IX * IY * 32), F32),
            pltpu.SemaphoreType.DMA((5,)),
        ],
        compiler_params=pltpu.CompilerParams(vmem_limit_bytes=LIMIT),
        cost_estimate=cost(11),
        name="kernel_grad",
    )(par, g, arr, da, db, sa, sb)


def swap(x, axis, phase):
    n = lax.axis_size(axis)
    pairs = []
    for i in range(phase, n - 1, 2):
        pairs += [(i, i + 1), (i + 1, i)]
    return lax.ppermute(x, axis, pairs)


def swap_space(one, two, da, db, odd_s, odd_d):
    def side(x):
        first_y = jnp.where(odd_d == 1, da[:, x], db[:, x])[:, None]
        last_y = jnp.where(odd_d == 1, db[:, x], da[:, x])[:, None]
        return jnp.concatenate([first_y, jnp.stack([one[x], two[x]]), last_y], 1)

    lo, hi = side(0), side(one.shape[0] - 1)
    to_a = jnp.where(odd_s == 1, lo, hi)
    to_b = jnp.where(odd_s == 1, hi, lo)
    return swap(to_a, "space", 0), swap(to_b, "space", 1)


def all_sum(x):
    for axis in ("depth", "space"):
        n = lax.axis_size(axis)
        step = 1
        while step < n:
            x = x + lax.ppermute(x, axis, [(i, i ^ step) for i in range(n)])
            step *= 2
    return x


def shards(features, occupancy, weight_one, weight_two, cotangent):
    mask = jnp.repeat(occupancy, BRICK, axis=2).astype(F32)[:, :, None, :]
    odd_s, odd_d = lax.axis_index("space") % 2, lax.axis_index("depth") % 2
    par = jnp.stack([odd_s, odd_d]).astype(jnp.int32)
    span = features.shape[0] * lax.axis_size("space")

    a_in, a_og, rim_a, rim_b = relayout(par, mask, features, cotangent)
    da, db = swap(rim_a, "depth", 0), swap(rim_b, "depth", 1)
    t1, t2b, t2, t1b = bands(weight_one, weight_two)
    sa, sb = swap_space(a_in, a_og, da, db, odd_s, odd_d)

    hid, pre, hrim_a, hrim_b = first(par, mask, t1, t2b, a_in, a_og, da, db, sa, sb)
    hda, hdb = swap(hrim_a, "depth", 0), swap(hrim_b, "depth", 1)
    g_one = kernel_grad(par, pre, a_in, da, db, sa, sb, 0)
    hsa, hsb = swap_space(hid, pre, hda, hdb, odd_s, odd_d)
    g_two = kernel_grad(par, hid, a_og, da, db, sa, sb, 1)
    grads = all_sum(jnp.stack([g_one, g_two]))
    output = second(par, mask, t2, hid, hda, hdb, hsa, hsb, 0)
    grad_input = second(par, mask, t1b, pre, hda, hdb, hsa, hsb, 1)

    grads = grads[..., :96].reshape(2, 3, 3, 32, 3, 32) / span
    grad_one = grads[0].transpose(2, 0, 3, 1, 4).reshape(32, 864)
    grad_two = grads[1][::-1, ::-1, :, ::-1].transpose(4, 0, 3, 1, 2).reshape(32, 864)
    return output, grad_input, grad_one, grad_two


def solution(mesh):
    field = P(("groups", "space"), None, "depth", None)
    in_specs = (field, P(("groups", "space"), "depth", None), P(), P(), field)
    out_specs = (field, field, P("groups", None), P("groups", None))
    return jax.shard_map(shards, mesh=mesh, in_specs=in_specs, out_specs=out_specs, check_vma=False)
```

```python
import functools

import jax
import jax.numpy as jnp
from jax import lax
from jax.experimental import pallas as pl
from jax.experimental.pallas import tpu as pltpu
from jax.sharding import PartitionSpec as P

BRICK = 8
BX, BY = 2, 4
IX, IY = BX + 2, BY + 2
BF = jnp.bfloat16
F32 = jnp.float32
VMEM = pltpu.VMEM
ANY = pl.ANY
LIMIT = 28 << 20
ROWS = 2 * BX


def cost(us):
    return pl.CostEstimate(flops=int(us * 1.1e9), bytes_accessed=1 << 20, transcendentals=0)


def lane_ids(shape):
    return lax.broadcasted_iota(jnp.int32, shape, len(shape) - 1)


HB = pl.BlockSpec(memory_space=ANY)
VM = pl.BlockSpec(memory_space=VMEM)
PARAMS = pltpu.CompilerParams(vmem_limit_bytes=LIMIT)


def is_odd(axis):
    return lax.rem(lax.axis_index(axis), 2) == 1


def by_parity(odd, low, high, ref_a, ref_b):
    @pl.when(odd)
    def _():
        ref_a(low)
        ref_b(high)

    @pl.when(jnp.logical_not(odd))
    def _():
        ref_a(high)
        ref_b(low)


def grid_of(arr_shape):
    size_x, width, size_y, size_z = arr_shape
    return (size_x + 2, size_y + 2, width, size_z)


def relayout_kernel(mask, feat, cot, p_in, p_og, rim_a, rim_b, perm, rims):
    step = pl.program_id(0)
    rows, width, size_y = feat.shape[:3]
    n = width * size_y

    @pl.when(step == 0)
    def _():
        row = lax.broadcasted_iota(jnp.int32, (n, n), 0)
        at = (row % width) * size_y + row // width
        perm[...] = jnp.where(lane_ids((n, n)) == at, 1.0, 0.0).astype(BF)

    brick_x = step * rows // BRICK
    for which, (src, dst) in enumerate(((feat, p_in), (cot, p_og))):
        for r in range(0, rows, 2):
            wide = jnp.concatenate([src[r + k].reshape(n, 128) for k in range(2)], 1)
            moved = jnp.dot(perm[...], wide, preferred_element_type=F32)
            for k in range(2):
                x = step * rows + r + k
                for brick_y in range(size_y // BRICK):
                    y = slice(1 + brick_y * BRICK, 1 + (brick_y + 1) * BRICK)
                    value = moved[brick_y * BRICK * width : (brick_y + 1) * BRICK * width]
                    value = value[:, k * 128 : (k + 1) * 128] * mask[brick_x, brick_y]
                    value = value.astype(BF).reshape(BRICK, width, 128)
                    dst[1 + x, y] = value
                    if brick_y == 0:
                        rims[0, which, r + k] = value[0]
                    if brick_y == size_y // BRICK - 1:
                        rims[1, which, r + k] = value[BRICK - 1]
    put_rims(rims, step, rim_a, rim_b)


def put_rims(rims, step, rim_a, rim_b):
    rows = rims.shape[2]

    def put(ref):
        def store(value):
            ref[:, pl.ds(step * rows, rows)] = value

        return store

    by_parity(is_odd("depth"), rims[0], rims[1], put(rim_a), put(rim_b))


def relayout(mask, feat, cot):
    size_x, width, size_y, size_z = feat.shape
    native = pl.BlockSpec((ROWS, width, size_y, size_z), lambda i: (i, 0, 0, 0))
    arr = jax.ShapeDtypeStruct(grid_of(feat.shape), BF)
    rim = jax.ShapeDtypeStruct((2, size_x, width, size_z), BF)
    return pl.pallas_call(
        relayout_kernel,
        grid=(size_x // ROWS,),
        in_specs=[VM, native, native],
        out_specs=[VM] * 4,
        out_shape=[arr, arr, rim, rim],
        scratch_shapes=[
            VMEM((width * size_y, width * size_y), BF),
            VMEM((2, 2, ROWS, width, size_z), BF),
        ],
        compiler_params=pltpu.CompilerParams(vmem_limit_bytes=60 << 20),
        cost_estimate=cost(5),
        name="relayout",
    )(mask, feat, cot)


def sides_kernel(one, two, da, db, after, to_a, to_b):
    size_x, size_y = one.shape[0] - 2, one.shape[1] - 2
    odd_s, odd_d = is_odd("space"), is_odd("depth")

    def lay(ref):
        def put(x):
            for which, src in enumerate((one, two)):
                ref[which, 1 : size_y + 1] = src[1 + x, 1 : size_y + 1]

            def first_y(rim):
                ref[:, 0] = rim[:, x]

            def last_y(rim):
                ref[:, size_y + 1] = rim[:, x]

            by_parity(odd_d, da, db, first_y, last_y)

        return put

    by_parity(odd_s, 0, size_x - 1, lay(to_a), lay(to_b))


def sides(one, two, da, db, after):
    size_x, size_y, width, size_z = one.shape
    shape = jax.ShapeDtypeStruct((2, size_y, width, size_z), BF)
    return pl.pallas_call(
        sides_kernel,
        in_specs=[VM] * 5,
        out_specs=[VM, VM],
        out_shape=[shape, shape],
        compiler_params=PARAMS,
        cost_estimate=cost(1.5),
        name="sides",
    )(one, two, da, db, after)


def place(acc, piece, lane, at):
    shift = (at - lane) % 128
    if shift:
        piece = pltpu.roll(piece, shift, 1)
    here = lane_ids(piece.shape) // 32 == (at % 128) // 32
    acc[at // 128] = jnp.where(here, piece, acc[at // 128])


def bands_kernel(w_ref, after, *outs, which, interleave):
    width = 32
    lanes = lane_ids((width, 128))

    square = (BY * width, BY * width)
    row = lax.broadcasted_iota(jnp.int32, square, 0)
    perm = jnp.where(lane_ids(square) == (row % BY) * width + row // BY, 1.0, 0.0).astype(BF)

    def band(pick, out, interleave):
        base = [[jnp.zeros((width, 128), F32) for _ in range(6)] for _ in range(3)]
        for dx in range(3):
            for dy in range(3):
                for dz in range(3):
                    at = (dx * IY + dy) * width
                    piece, lane = pick((dx * 3 + dy) * 3 + dz)
                    place(base[dz], piece, lane, at)
        zero = jnp.zeros((width, 128), F32)
        for dz in range(3):
            turned = {0: base[dz]}
            for q in range(1, 4):
                rolled = [pltpu.roll(b, q * width, 1) for b in base[dz]]
                turned[q] = [
                    jnp.where(lanes < q * width, rolled[k - 1] if k else zero, rolled[k])
                    for k in range(6)
                ]
            for xo in range(BX):
                for k in range(6):
                    group = []
                    for yo in range(BY):
                        off = xo * IY + yo
                        moved, part = off // 4, off % 4
                        group.append(turned[part][k - moved] if k >= moved else zero)
                    group = jnp.concatenate(group, 0).astype(BF)
                    if interleave:
                        group = jnp.dot(perm, group, preferred_element_type=F32).astype(BF)
                    row = (dz * BX + xo) * BY * width
                    out[row : row + BY * width, k * 128 : (k + 1) * 128] = group

    def straight(which):
        def pick(tap):
            lane = tap * width
            col = lane // 128 * 128
            return w_ref[which, :, col : col + 128], lane % 128

        return pick

    def flipped(which):
        pad = jnp.zeros((128 - width, 896), F32)
        turned = jnp.concatenate([w_ref[which], pad], 0).T

        def pick(tap):
            back = 26 - tap
            return turned[back * width : (back + 1) * width], 0

        return pick

    band(straight(which), outs[0], interleave)
    band(flipped(1 - which), outs[1], interleave)


def bands(w, which, interleave, after):
    shape = jax.ShapeDtypeStruct((3 * BX * BY * 32, IX * IY * 32), BF)
    return pl.pallas_call(
        functools.partial(bands_kernel, which=which, interleave=interleave),
        in_specs=[VM, VM],
        out_specs=[VM] * 2,
        out_shape=[shape] * 2,
        compiler_params=pltpu.CompilerParams(vmem_limit_bytes=LIMIT),
        cost_estimate=cost(3),
        name="bands",
    )(w, after)


def lay_rims(padded, which, da, db, sa, sb):
    size_x, size_y = padded.shape[0] - 2, padded.shape[1] - 2
    spot_da = jnp.where(is_odd("depth"), 0, size_y + 1)
    spot_sa = jnp.where(is_odd("space"), 0, size_x + 1)
    padded[1 : size_x + 1, pl.ds(spot_da, 1)] = da[which][:, None]
    padded[1 : size_x + 1, pl.ds(size_y + 1 - spot_da, 1)] = db[which][:, None]
    padded[pl.ds(spot_sa, 1)] = sa[which][None]
    padded[pl.ds(size_x + 1 - spot_sa, 1)] = sb[which][None]


def block_input(padded, bx, pair):
    parts = []
    for by in (2 * pair, 2 * pair + 1):
        part = padded[pl.ds(BX * bx, IX), BY * by : BY * by + IY]
        parts.append(part.reshape(IX * IY * 32, 128))
    return jnp.concatenate(parts, 1)


def z_sum(product, half):
    n = BX * BY * 32
    p = product[:, half * 128 : (half + 1) * 128]
    lanes = lane_ids((n, 128))
    below = jnp.where(lanes > 0, pltpu.roll(p[:n], 1, 1), 0.0)
    above = jnp.where(lanes < 127, pltpu.roll(p[2 * n :], 127, 1), 0.0)
    return p[n : 2 * n] + below + above


def first_kernel(
    mask, t_one, t_two, in_0, og_0, da, db, sa, sb, p_in, p_og, hid, pre, rim_a, rim_b, rims
):
    step = pl.program_id(0)
    size_y = hid.shape[1] - 2

    @pl.when(step == 0)
    def _():
        lay_rims(p_in, 0, da, db, sa, sb)
        lay_rims(p_og, 1, da, db, sa, sb)

    for sub in range(ROWS // BX):
        bx = step * (ROWS // BX) + sub
        x = pl.ds(1 + bx * BX, BX)
        for pair in range(size_y // (2 * BY)):
            one = jnp.dot(t_one[...], block_input(p_in, bx, pair), preferred_element_type=F32)
            two = jnp.dot(t_two[...], block_input(p_og, bx, pair), preferred_element_type=F32)
            for half in range(2):
                by = 2 * pair + half
                m = mask[bx * BX // BRICK, by * BY // BRICK]
                act = z_sum(one, half)
                grad = z_sum(two, half)
                sig = 1.0 / (1.0 + jnp.exp(-act))
                hidden = (act * sig * m).astype(BF).reshape(BX, BY, 32, 128)
                slope = (grad * sig * (1.0 + act * (1.0 - sig)) * m).astype(BF)
                slope = slope.reshape(BX, BY, 32, 128)
                y = slice(1 + by * BY, 1 + (by + 1) * BY)
                for which, (ref, value) in enumerate(((hid, hidden), (pre, slope))):
                    ref[x, y] = value
                    if by == 0:
                        rims[0, which, sub * BX : (sub + 1) * BX] = value[:, 0]
                    if by == size_y // BY - 1:
                        rims[1, which, sub * BX : (sub + 1) * BX] = value[:, BY - 1]
    put_rims(rims, step, rim_a, rim_b)


def first(mask, t_one, t_two, p_in, p_og, da, db, sa, sb):
    width, size_z = p_in.shape[2:]
    arr = jax.ShapeDtypeStruct(p_in.shape, BF)
    rim_shape = jax.ShapeDtypeStruct(da.shape, BF)
    return pl.pallas_call(
        first_kernel,
        grid=((p_in.shape[0] - 2) // ROWS,),
        in_specs=[VM] * 9,
        out_specs=[VM] * 6,
        out_shape=[arr] * 4 + [rim_shape] * 2,
        input_output_aliases={3: 0, 4: 1},
        scratch_shapes=[VMEM((2, 2, ROWS, width, size_z), BF)],
        compiler_params=PARAMS,
        cost_estimate=cost(16),
        name="first",
    )(mask, t_one, t_two, p_in, p_og, da, db, sa, sb)


def second_kernel(mask, t, arr, after, *rest, which, start):
    padded, out = rest[-2:]
    step = pl.program_id(0)
    width, size_y = out.shape[1], out.shape[2]
    if len(rest) == 6:

        @pl.when(step == 0)
        def _():
            lay_rims(padded, which, *rest[:4])

    low_half = lax.broadcasted_iota(jnp.int32, (BX * width // 2, 8, 128), 1) < BY
    for sub in range(ROWS // BX):
        bx = (step + start) * (ROWS // BX) + sub
        pairs = []
        for pair in range(size_y // (2 * BY)):
            product = jnp.dot(t[...], block_input(padded, bx, pair), preferred_element_type=F32)
            m = mask[bx * BX // BRICK, pair * 2 * BY // BRICK]
            left, right = [(z_sum(product, h) * m).reshape(low_half.shape) for h in range(2)]
            even = jnp.where(low_half, left, pltpu.roll(right, BY, 1))
            odd = jnp.where(low_half, pltpu.roll(left, BY, 1), right)
            both = jnp.stack([even, odd], 1)
            pairs.append(both.reshape(BX, width, 8, 128))
        out[sub * BX : (sub + 1) * BX] = jnp.concatenate(pairs, 2).astype(BF)


def second(mask, t, padded, rims, which, after, start=0, steps=None, onto=None):
    size_x, size_y, width, size_z = padded.shape
    size_x, size_y = size_x - 2, size_y - 2
    steps = steps or size_x // ROWS
    native = pl.BlockSpec((ROWS, width, size_y, size_z), lambda i: (i + start, 0, 0, 0))
    args = (mask, t, padded, after) + (tuple(rims) if onto is None else (onto,))
    return pl.pallas_call(
        functools.partial(second_kernel, which=which, start=start),
        grid=(steps,),
        in_specs=[VM] * 4 + ([VM] * 4 if onto is None else [HB]),
        out_specs=[VM, native],
        out_shape=[
            jax.ShapeDtypeStruct(padded.shape, BF),
            jax.ShapeDtypeStruct((size_x, width, size_y, size_z), BF),
        ],
        input_output_aliases={2: 0} if onto is None else {2: 0, 4: 1},
        compiler_params=PARAMS,
        cost_estimate=cost(2.5 * steps),
        name="second",
    )(*args)


def grad_sum(step, g, padded, total):
    size_y = g.shape[1] - 2
    n = BX * BY * 32
    lhs, rhs = [], []
    for sub in range(ROWS // BX):
        bx = step * (ROWS // BX) + sub
        for by in range(size_y // BY):
            x, y = pl.ds(1 + bx * BX, BX), slice(1 + by * BY, 1 + (by + 1) * BY)
            block = g[x, y].reshape(n, 128).astype(F32)
            lanes = lane_ids((n, 128))
            ahead = jnp.where(lanes < 127, pltpu.roll(block, 127, 1), 0.0)
            behind = jnp.where(lanes > 0, pltpu.roll(block, 1, 1), 0.0)
            lhs.append(jnp.concatenate([ahead, block, behind], 0).astype(BF))
        rhs += [block_input(padded, bx, p) for p in range(size_y // (2 * BY))]
    lhs, rhs = jnp.concatenate(lhs, 1), jnp.concatenate(rhs, 1)
    product = lax.dot_general(lhs, rhs, (((1,), (1,)), ((), ())), preferred_element_type=F32)

    @pl.when(step == 0)
    def _():
        total[...] = product

    @pl.when(step > 0)
    def _():
        total[...] += product


def grad_taps(total, out):
    lanes = IX * IY * 32
    for dz in range(3):
        acc = jnp.zeros((32, lanes), F32)
        for xo in range(BX):
            for yo in range(BY):
                row = ((dz * BX + xo) * BY + yo) * 32
                part = total[row : row + 32, :]
                shift = (xo * IY + yo) * 32
                acc += pltpu.roll(part, lanes - shift, 1) if shift else part
        for dx in range(3):
            at = dx * IY * 32
            moved = pltpu.roll(acc, lanes - at, 1) if at else acc
            out[dx, dz * 32 : (dz + 1) * 32, :] = moved[:, :128]


def grad_one_kernel(g, padded, out, total):
    step = pl.program_id(0)
    grad_sum(step, g, padded, total)

    @pl.when(step == pl.num_programs(0) - 1)
    def _():
        grad_taps(total, out)


def grad_two_kernel(g, padded, one, after, keep, send, taps, total):
    step = pl.program_id(0)
    grad_sum(step, g, padded, total)

    @pl.when(step == pl.num_programs(0) - 1)
    def _():
        grad_taps(total, taps)

        def store(ref):
            def put(value):
                ref[...] = value

            return put

        by_parity(is_odd("depth"), taps[...], one[...], store(keep), store(send))


def kernel_grad(kernel, g, padded, extra=(), outs=1, scratch=()):
    taps = jax.ShapeDtypeStruct((3, 96, 128), F32)
    return pl.pallas_call(
        kernel,
        grid=((padded.shape[0] - 2) // ROWS,),
        in_specs=[VM] * (2 + len(extra)),
        out_specs=[VM] * outs,
        out_shape=[taps] * outs,
        scratch_shapes=list(scratch) + [VMEM((3 * BX * BY * 32, IX * IY * 32), F32)],
        compiler_params=PARAMS,
        cost_estimate=cost(9),
        name="kernel_grad",
    )(g, padded, *extra)


def finish_kernel(own, other, out_one, out_two, *, span):
    def zeros():
        return [jnp.zeros((32, 128), F32) for _ in range(7)]

    def write(acc, out):
        for k in range(7):
            end = min((k + 1) * 128, out.shape[1])
            out[:, k * 128 : end] = acc[k][:, : end - k * 128] / span

    def both(one, two):
        acc = zeros()
        for dx in range(3):
            for dz in range(3):
                block = one[dx, dz * 32 : (dz + 1) * 32, :]
                for dy in range(3):
                    place(acc, block, dy * 32, ((dx * 3 + dy) * 3 + dz) * 32)
        write(acc, out_one)
        acc = zeros()
        pad = jnp.zeros((96, 128), F32)
        for dx in range(3):
            for dz in range(3):
                block = two[dx, dz * 32 : (dz + 1) * 32, :]
                turned = jnp.concatenate([block, pad], 0).T
                for dy in range(3):
                    tap = ((2 - dx) * 3 + 2 - dy) * 3 + 2 - dz
                    place(acc, turned[dy * 32 : (dy + 1) * 32], 0, tap * 32)
        write(acc, out_two)

    odd = is_odd("depth")

    @pl.when(odd)
    def _():
        both(other, own)

    @pl.when(jnp.logical_not(odd))
    def _():
        both(own, other)


def finish(own, other, span):
    shape = jax.ShapeDtypeStruct((32, 864), F32)
    return pl.pallas_call(
        functools.partial(finish_kernel, span=span),
        in_specs=[VM] * 2,
        out_specs=[VM] * 2,
        out_shape=[shape, shape],
        compiler_params=PARAMS,
        cost_estimate=cost(2),
        name="finish",
    )(own, other)


def swap(x, axis, phase):
    n = lax.axis_size(axis)
    pairs = []
    for i in range(phase, n - 1, 2):
        pairs += [(i, i + 1), (i + 1, i)]
    return lax.ppermute(x, axis, pairs)


def both_phases(to_a, to_b, axis):
    return swap(to_a, axis, 0), swap(to_b, axis, 1)


def add_kernel(x, y, after, out):
    out[...] = x[...] + y[...]


def add_after(x, y, after):
    return pl.pallas_call(
        add_kernel,
        in_specs=[VM, VM, VM],
        out_specs=VM,
        out_shape=jax.ShapeDtypeStruct(x.shape, x.dtype),
        compiler_params=PARAMS,
        cost_estimate=cost(1),
        name="add_after",
    )(x, y, after)


def partner(x, axis, step):
    return lax.ppermute(x, axis, [(i, i ^ step) for i in range(lax.axis_size(axis))])


def shards(features, occupancy, weight_one, weight_two, cotangent):
    mask = jnp.repeat(occupancy, BRICK, axis=2).astype(F32)[:, :, None, :]
    span = features.shape[0] * lax.axis_size("space")
    w = jnp.stack([weight_one, weight_two]).astype(F32)
    w = jnp.pad(w, ((0, 0), (0, 0), (0, 896 - w.shape[2])))

    p_in, p_og, rim_a, rim_b = relayout(mask, features, cotangent)
    da, db = both_phases(rim_a, rim_b, "depth")
    t1, t2b = bands(w, 0, False, rim_a)
    to_a, to_b = sides(p_in, p_og, da, db, t1)
    sa, sb = both_phases(to_a, to_b, "space")
    t2, t1b = bands(w, 1, True, to_a)

    p_in, p_og, hid, pre, rim_a, rim_b = first(mask, t1, t2b, p_in, p_og, da, db, sa, sb)
    da, db = both_phases(rim_a, rim_b, "depth")
    (g_one,) = kernel_grad(grad_one_kernel, pre, p_in)
    to_a, to_b = sides(hid, pre, da, db, g_one)
    sa, sb = both_phases(to_a, to_b, "space")
    taps = VMEM((3, 96, 128), F32)
    keep, send = kernel_grad(grad_two_kernel, hid, p_og, (g_one, to_a), 2, [taps])
    rims = (da, db, sa, sb)
    total = keep + swap(send, "depth", 0)
    steps = [("depth", 1 << k) for k in range(1, lax.axis_size("depth").bit_length() - 1)]
    steps += [("space", 1 << k) for k in range(lax.axis_size("space").bit_length() - 1)]
    received = partner(total, *steps[0])
    hid, output = second(mask, t2, hid, rims, 0, total)
    total = add_after(total, received, hid)
    received = partner(total, *steps[1])
    pre, half = second(mask, t1b, pre, rims, 1, total, 0, 2)
    total = add_after(total, received, pre)
    received = partner(total, *steps[2])
    pre, grad_input = second(mask, t1b, pre, rims, 1, total, 2, 2, half)
    total = add_after(total, received, pre)
    for step in steps[3:]:
        total = total + partner(total, *step)
    grad_one, grad_two = finish(total, swap(total, "depth", 0), span)
    return output, grad_input, grad_one, grad_two


def solution(mesh):
    field = P(("groups", "space"), None, "depth", None)
    in_specs = (field, P(("groups", "space"), "depth", None), P(), P(), field)
    out_specs = (field, field, P("groups", None), P("groups", None))
    return jax.shard_map(shards, mesh=mesh, in_specs=in_specs, out_specs=out_specs, check_vma=False)
```

```python
import functools

import jax
import jax.numpy as jnp
from jax import lax
from jax.experimental import pallas as pl
from jax.experimental.pallas import tpu as pltpu
from jax.sharding import PartitionSpec as P

BRICK = 8
BX, BY = 2, 4
IX, IY = BX + 2, BY + 2
BF = jnp.bfloat16
F32 = jnp.float32
VMEM = pltpu.VMEM
ANY = pl.ANY
LIMIT = 28 << 20


def cost(us):
    return pl.CostEstimate(flops=int(us * 1.1e9), bytes_accessed=1 << 20, transcendentals=0)


def lane_ids(shape):
    return lax.broadcasted_iota(jnp.int32, shape, len(shape) - 1)


HB = pl.BlockSpec(memory_space=ANY)
VM = pl.BlockSpec(memory_space=VMEM)
PARAMS = pltpu.CompilerParams(vmem_limit_bytes=LIMIT)


def is_odd(axis):
    return lax.rem(lax.axis_index(axis), 2) == 1


def by_parity(odd, low, high, ref_a, ref_b):
    @pl.when(odd)
    def _():
        ref_a(low)
        ref_b(high)

    @pl.when(jnp.logical_not(odd))
    def _():
        ref_a(high)
        ref_b(low)


def grid_of(arr_shape):
    size_x, width, size_y, size_z = arr_shape
    return (size_x + 2, size_y + 2, width, size_z)


def mask_kernel(occ, mask, perm):
    lanes = lane_ids((1, 128)) // BRICK
    for i in range(occ.shape[0]):
        for j in range(occ.shape[1]):
            row = jnp.zeros((1, 128), F32)
            for k in range(occ.shape[2]):
                row = jnp.where(lanes == k, occ[i, j, k].astype(F32), row)
            mask[i, j] = row
    n = perm.shape[0]
    size_y = n // 32
    row = lax.broadcasted_iota(jnp.int32, (n, n), 0)
    at = (row % 32) * size_y + row // 32
    perm[...] = jnp.where(lane_ids((n, n)) == at, 1.0, 0.0).astype(BF)


def masks(occ, size_y, size_z):
    n = 32 * size_y
    return pl.pallas_call(
        mask_kernel,
        in_specs=[pl.BlockSpec(memory_space=pltpu.SMEM)],
        out_specs=[VM] * 2,
        out_shape=[
            jax.ShapeDtypeStruct((*occ.shape[:2], 1, size_z), F32),
            jax.ShapeDtypeStruct((n, n), BF),
        ],
        compiler_params=PARAMS,
        cost_estimate=cost(0.5),
        name="masks",
    )(occ)


def relayout_kernel(mask, perm, feat, dst):
    size_x, width, size_y = feat.shape[:3]
    n = width * size_y
    for x in range(0, size_x, 2):
        wide = jnp.concatenate([feat[x + k].reshape(n, 128) for k in range(2)], 1)
        moved = jnp.dot(perm[...], wide, preferred_element_type=F32)
        for k in range(2):
            for brick_y in range(size_y // BRICK):
                y = slice(1 + brick_y * BRICK, 1 + (brick_y + 1) * BRICK)
                value = moved[brick_y * BRICK * width : (brick_y + 1) * BRICK * width]
                value = value[:, k * 128 : (k + 1) * 128] * mask[x // BRICK, brick_y]
                dst[1 + x + k, y] = value.astype(BF).reshape(BRICK, width, 128)


def relayout(mask, perm, feat):
    return pl.pallas_call(
        relayout_kernel,
        in_specs=[VM] * 3,
        out_specs=VM,
        out_shape=jax.ShapeDtypeStruct(grid_of(feat.shape), BF),
        compiler_params=PARAMS,
        cost_estimate=cost(2),
        name="relayout",
    )(mask, perm, feat)


def y_rims_kernel(one, two, to_a, to_b):
    size_x, size_y = one.shape[0] - 2, one.shape[1] - 2

    def lay(ref):
        def put(y):
            for which, src in enumerate((one, two)):
                ref[which] = src[1 : size_x + 1, y]

        return put

    by_parity(is_odd("depth"), 1, size_y, lay(to_a), lay(to_b))


def x_rims_kernel(one, two, after, to_a, to_b):
    def lay(ref):
        def put(x):
            for which, src in enumerate((one, two)):
                ref[which] = src[x]

        return put

    by_parity(is_odd("space"), 1, one.shape[0] - 2, lay(to_a), lay(to_b))


def rims(kernel, name, length, one, two, *after):
    shape = jax.ShapeDtypeStruct((2, length, *one.shape[2:]), BF)
    return pl.pallas_call(
        kernel,
        in_specs=[VM] * (2 + len(after)),
        out_specs=[VM, VM],
        out_shape=[shape, shape],
        compiler_params=PARAMS,
        cost_estimate=cost(0.1),
        name=name,
    )(one, two, *after)


def lay_y_kernel(one, two, da, db, after, one_out, two_out):
    size_x, size_y = one.shape[0] - 2, one.shape[1] - 2
    spot = jnp.where(is_odd("depth"), 0, size_y + 1)
    for which, dst in enumerate((one_out, two_out)):
        dst[1 : size_x + 1, pl.ds(spot, 1)] = da[which][:, None]
        dst[1 : size_x + 1, pl.ds(size_y + 1 - spot, 1)] = db[which][:, None]


def lay_x_kernel(one, two, sa, sb, after, one_out, two_out):
    size_x = one.shape[0] - 2
    spot = jnp.where(is_odd("space"), 0, size_x + 1)
    for which, dst in enumerate((one_out, two_out)):
        dst[pl.ds(spot, 1)] = sa[which][None]
        dst[pl.ds(size_x + 1 - spot, 1)] = sb[which][None]


def lay(kernel, name, one, two, got_a, got_b, after):
    shape = jax.ShapeDtypeStruct(one.shape, BF)
    return pl.pallas_call(
        kernel,
        in_specs=[VM] * 5,
        out_specs=[VM, VM],
        out_shape=[shape, shape],
        input_output_aliases={0: 0, 1: 1},
        compiler_params=PARAMS,
        cost_estimate=cost(0.1),
        name=name,
    )(one, two, got_a, got_b, after)


def place(acc, piece, lane, at):
    shift = (at - lane) % 128
    if shift:
        piece = pltpu.roll(piece, shift, 1)
    here = lane_ids(piece.shape) // 32 == (at % 128) // 32
    acc[at // 128] = jnp.where(here, piece, acc[at // 128])


def bands_kernel(w_ref, after, *outs, which, interleave):
    width = 32
    lanes = lane_ids((width, 128))

    square = (BY * width, BY * width)
    row = lax.broadcasted_iota(jnp.int32, square, 0)
    perm = jnp.where(lane_ids(square) == (row % BY) * width + row // BY, 1.0, 0.0).astype(BF)

    def band(pick, out, interleave):
        base = [[jnp.zeros((width, 128), F32) for _ in range(6)] for _ in range(3)]
        for dx in range(3):
            for dy in range(3):
                for dz in range(3):
                    at = (dx * IY + dy) * width
                    piece, lane = pick((dx * 3 + dy) * 3 + dz)
                    place(base[dz], piece, lane, at)
        zero = jnp.zeros((width, 128), F32)
        for dz in range(3):
            turned = {0: base[dz]}
            for q in range(1, 4):
                rolled = [pltpu.roll(b, q * width, 1) for b in base[dz]]
                turned[q] = [
                    jnp.where(lanes < q * width, rolled[k - 1] if k else zero, rolled[k])
                    for k in range(6)
                ]
            for xo in range(BX):
                for k in range(6):
                    group = []
                    for yo in range(BY):
                        off = xo * IY + yo
                        moved, part = off // 4, off % 4
                        group.append(turned[part][k - moved] if k >= moved else zero)
                    group = jnp.concatenate(group, 0).astype(BF)
                    if interleave:
                        group = jnp.dot(perm, group, preferred_element_type=F32).astype(BF)
                    row = (dz * BX + xo) * BY * width
                    out[row : row + BY * width, k * 128 : (k + 1) * 128] = group

    def straight(which):
        def pick(tap):
            lane = tap * width
            col = lane // 128 * 128
            return w_ref[which, :, col : col + 128], lane % 128

        return pick

    def flipped(which):
        pad = jnp.zeros((128 - width, 896), F32)
        turned = jnp.concatenate([w_ref[which], pad], 0).T

        def pick(tap):
            back = 26 - tap
            return turned[back * width : (back + 1) * width], 0

        return pick

    band(straight(which), outs[0], interleave)
    band(flipped(1 - which), outs[1], interleave)


def bands(w, which, interleave, after):
    shape = jax.ShapeDtypeStruct((3 * BX * BY * 32, IX * IY * 32), BF)
    return pl.pallas_call(
        functools.partial(bands_kernel, which=which, interleave=interleave),
        in_specs=[VM, VM],
        out_specs=[VM] * 2,
        out_shape=[shape] * 2,
        compiler_params=pltpu.CompilerParams(vmem_limit_bytes=LIMIT),
        cost_estimate=cost(3),
        name="bands",
    )(w, after)


def block_input(padded, bx, pair):
    parts = []
    for by in pair:
        part = padded[pl.ds(BX * bx, IX), BY * by : BY * by + IY]
        parts.append(part.reshape(IX * IY * 32, 128))
    return jnp.concatenate(parts, 1)


def z_sum(product, half):
    n = BX * BY * 32
    p = product[:, half * 128 : (half + 1) * 128]
    lanes = lane_ids((n, 128))
    below = jnp.where(lanes > 0, pltpu.roll(p[:n], 1, 1), 0.0)
    above = jnp.where(lanes < 127, pltpu.roll(p[2 * n :], 127, 1), 0.0)
    return p[n : 2 * n] + below + above


def first_kernel(mask, t_one, t_two, p_in, p_og, *rest, edge, pairs):
    hid, pre = rest[-2:]
    last = (hid.shape[0] - 2) // BX - 1
    bxs = (0, last) if edge else range(1, last)
    for bx in bxs:
        x = pl.ds(1 + bx * BX, BX)
        for pair in pairs:
            one = jnp.dot(t_one[...], block_input(p_in, bx, pair), preferred_element_type=F32)
            two = jnp.dot(t_two[...], block_input(p_og, bx, pair), preferred_element_type=F32)
            for half, by in enumerate(pair):
                m = mask[bx * BX // BRICK, by * BY // BRICK]
                act = z_sum(one, half)
                grad = z_sum(two, half)
                sig = 1.0 / (1.0 + jnp.exp(-act))
                hidden = (act * sig * m).astype(BF)
                slope = (grad * sig * (1.0 + act * (1.0 - sig)) * m).astype(BF)
                y = slice(1 + by * BY, 1 + (by + 1) * BY)
                hid[x, y] = hidden.reshape(BX, BY, 32, 128)
                pre[x, y] = slope.reshape(BX, BY, 32, 128)


def first(mask, t_one, t_two, p_in, p_og, onto, edge, pairs):
    arr = jax.ShapeDtypeStruct(p_in.shape, BF)
    return pl.pallas_call(
        functools.partial(first_kernel, edge=edge, pairs=pairs),
        in_specs=[VM] * (5 + len(onto)),
        out_specs=[VM] * 2,
        out_shape=[arr] * 2,
        input_output_aliases={5: 0, 6: 1} if onto else {},
        compiler_params=PARAMS,
        cost_estimate=cost(5),
        name="first",
    )(mask, t_one, t_two, p_in, p_og, *onto)


def second_kernel(mask, t, padded, after, *rest, edge):
    out, token, held, sem = rest[-4:]
    width, size_y = out.shape[1], out.shape[2]
    token[...] = jnp.zeros_like(token)
    last = out.shape[0] // BX - 1
    bxs = (0, 1, last - 1, last) if edge else range(2, last - 1)
    low_half = lax.broadcasted_iota(jnp.int32, (BX * width // 2, 8, 128), 1) < BY
    copies = []
    for slot, bx in enumerate(bxs):
        pairs = []
        for at in range(0, size_y // BY, 2):
            pair = (at, at + 1)
            product = jnp.dot(t[...], block_input(padded, bx, pair), preferred_element_type=F32)
            m = mask[bx * BX // BRICK, at * BY // BRICK]
            left, right = [(z_sum(product, h) * m).reshape(low_half.shape) for h in range(2)]
            even = jnp.where(low_half, left, pltpu.roll(right, BY, 1))
            odd = jnp.where(low_half, pltpu.roll(left, BY, 1), right)
            both = jnp.stack([even, odd], 1)
            pairs.append(both.reshape(BX, width, 8, 128))
        held[slot] = jnp.concatenate(pairs, 2).astype(BF)
        made = pltpu.make_async_copy(held.at[slot], out.at[pl.ds(bx * BX, BX)], sem.at[slot])
        made.start()
        copies.append(made)
    for made in copies:
        made.wait()


def second(mask, t, padded, after, edge, onto=(), us=4):
    size_x, size_y, width, size_z = padded.shape
    size_x, size_y = size_x - 2, size_y - 2
    slots = 4 if edge else size_x // BX - 4
    return pl.pallas_call(
        functools.partial(second_kernel, edge=edge),
        in_specs=[VM] * 4 + [HB] * len(onto),
        out_specs=[HB, VM],
        out_shape=[
            jax.ShapeDtypeStruct((size_x, width, size_y, size_z), BF),
            jax.ShapeDtypeStruct((8, 128), F32),
        ],
        input_output_aliases={4: 0} if onto else {},
        scratch_shapes=[
            VMEM((slots, BX, width, size_y, size_z), BF),
            pltpu.SemaphoreType.DMA((slots,)),
        ],
        compiler_params=PARAMS,
        cost_estimate=cost(us),
        name="second",
    )(mask, t, padded, after, *onto)


def grad_sum(g, padded, total):
    size_y = g.shape[1] - 2
    n = BX * BY * 32
    lhs, rhs = [], []
    for bx in range((g.shape[0] - 2) // BX):
        for by in range(size_y // BY):
            x, y = pl.ds(1 + bx * BX, BX), slice(1 + by * BY, 1 + (by + 1) * BY)
            block = g[x, y].reshape(n, 128).astype(F32)
            lanes = lane_ids((n, 128))
            ahead = jnp.where(lanes < 127, pltpu.roll(block, 127, 1), 0.0)
            behind = jnp.where(lanes > 0, pltpu.roll(block, 1, 1), 0.0)
            lhs.append(jnp.concatenate([ahead, block, behind], 0).astype(BF))
        rhs += [block_input(padded, bx, (at, at + 1)) for at in range(0, size_y // BY, 2)]
    lhs, rhs = jnp.concatenate(lhs, 1), jnp.concatenate(rhs, 1)
    total[...] = lax.dot_general(lhs, rhs, (((1,), (1,)), ((), ())), preferred_element_type=F32)


def grad_taps(total, out):
    lanes = IX * IY * 32
    for dz in range(3):
        acc = jnp.zeros((32, lanes), F32)
        for xo in range(BX):
            for yo in range(BY):
                row = ((dz * BX + xo) * BY + yo) * 32
                part = total[row : row + 32, :]
                shift = (xo * IY + yo) * 32
                acc += pltpu.roll(part, lanes - shift, 1) if shift else part
        for dx in range(3):
            at = dx * IY * 32
            moved = pltpu.roll(acc, lanes - at, 1) if at else acc
            out[dx, dz * 32 : (dz + 1) * 32, :] = moved[:, :128]


def grad_one_kernel(g, padded, out, total):
    grad_sum(g, padded, total)
    grad_taps(total, out)


def grad_two_kernel(g, padded, one, after, keep, send, taps, total):
    grad_sum(g, padded, total)
    grad_taps(total, taps)

    def store(ref):
        def put(value):
            ref[...] = value

        return put

    by_parity(is_odd("depth"), taps[...], one[...], store(keep), store(send))


def kernel_grad(kernel, g, padded, extra=(), outs=1, scratch=()):
    taps = jax.ShapeDtypeStruct((3, 96, 128), F32)
    return pl.pallas_call(
        kernel,
        in_specs=[VM] * (2 + len(extra)),
        out_specs=[VM] * outs,
        out_shape=[taps] * outs,
        scratch_shapes=list(scratch) + [VMEM((3 * BX * BY * 32, IX * IY * 32), F32)],
        compiler_params=PARAMS,
        cost_estimate=cost(8),
        name="kernel_grad",
    )(g, padded, *extra)


def finish_kernel(own, other, out_one, out_two, *, span):
    def zeros():
        return [jnp.zeros((32, 128), F32) for _ in range(7)]

    def write(acc, out):
        for k in range(7):
            end = min((k + 1) * 128, out.shape[1])
            out[:, k * 128 : end] = acc[k][:, : end - k * 128] / span

    def both(one, two):
        acc = zeros()
        for dx in range(3):
            for dz in range(3):
                block = one[dx, dz * 32 : (dz + 1) * 32, :]
                for dy in range(3):
                    place(acc, block, dy * 32, ((dx * 3 + dy) * 3 + dz) * 32)
        write(acc, out_one)
        acc = zeros()
        pad = jnp.zeros((96, 128), F32)
        for dx in range(3):
            for dz in range(3):
                block = two[dx, dz * 32 : (dz + 1) * 32, :]
                turned = jnp.concatenate([block, pad], 0).T
                for dy in range(3):
                    tap = ((2 - dx) * 3 + 2 - dy) * 3 + 2 - dz
                    place(acc, turned[dy * 32 : (dy + 1) * 32], 0, tap * 32)
        write(acc, out_two)

    odd = is_odd("depth")

    @pl.when(odd)
    def _():
        both(other, own)

    @pl.when(jnp.logical_not(odd))
    def _():
        both(own, other)


def finish(own, other, span):
    shape = jax.ShapeDtypeStruct((32, 864), F32)
    return pl.pallas_call(
        functools.partial(finish_kernel, span=span),
        in_specs=[VM] * 2,
        out_specs=[VM] * 2,
        out_shape=[shape, shape],
        compiler_params=PARAMS,
        cost_estimate=cost(2),
        name="finish",
    )(own, other)


def swap(x, axis, phase):
    n = lax.axis_size(axis)
    pairs = []
    for i in range(phase, n - 1, 2):
        pairs += [(i, i + 1), (i + 1, i)]
    return lax.ppermute(x, axis, pairs)


def both_phases(to_a, to_b, axis):
    return swap(to_a, axis, 0), swap(to_b, axis, 1)


def add_kernel(x, y, after, out):
    out[...] = (x[...].astype(F32) + y[...].astype(F32)).astype(out.dtype)


def add_after(x, y, after, dtype=F32):
    return pl.pallas_call(
        add_kernel,
        in_specs=[VM, VM, VM],
        out_specs=VM,
        out_shape=jax.ShapeDtypeStruct(x.shape, dtype),
        compiler_params=PARAMS,
        cost_estimate=cost(0.1),
        name="add_after",
    )(x, y, after)


def partner(x, axis, step):
    return lax.ppermute(x, axis, [(i, i ^ step) for i in range(lax.axis_size(axis))])


def shards(features, occupancy, weight_one, weight_two, cotangent):
    span = features.shape[0] * lax.axis_size("space")
    w = jnp.stack([weight_one, weight_two]).astype(F32)
    w = jnp.pad(w, ((0, 0), (0, 0), (0, 896 - w.shape[2])))

    size_x, size_y = features.shape[0], features.shape[2]
    by = range(size_y // BY)
    middle, ends = [by[k : k + 2] for k in by[1:-1:2]], [(by[0], by[-1])]

    mask, perm = masks(occupancy, size_y, features.shape[3])
    p_in = relayout(mask, perm, features)
    p_og = relayout(mask, perm, cotangent)
    da, db = both_phases(*rims(y_rims_kernel, "y_rims", size_x, p_in, p_og), "depth")
    t1, t2b = bands(w, 0, False, p_in)
    t2, t1b = bands(w, 1, True, p_in)
    out = first(mask, t1, t2b, p_in, p_og, (), False, middle)
    p_in, p_og = lay(lay_y_kernel, "lay_y", p_in, p_og, da, db, out[0])
    to_a, to_b = rims(x_rims_kernel, "x_rims", size_y + 2, p_in, p_og, t2)
    sa, sb = both_phases(to_a, to_b, "space")
    out = first(mask, t1, t2b, p_in, p_og, out, False, ends)
    p_in, p_og = lay(lay_x_kernel, "lay_x", p_in, p_og, sa, sb, out[0])
    hid, pre = first(mask, t1, t2b, p_in, p_og, out, True, middle + ends)

    da, db = both_phases(*rims(y_rims_kernel, "y_rims", size_x, hid, pre), "depth")
    (g_one,) = kernel_grad(grad_one_kernel, pre, p_in)
    hid, pre = lay(lay_y_kernel, "lay_y", hid, pre, da, db, g_one)
    to_a, to_b = rims(x_rims_kernel, "x_rims", size_y + 2, hid, pre, g_one)
    sa, sb = both_phases(to_a, to_b, "space")
    taps = VMEM((3, 96, 128), F32)
    keep, send = kernel_grad(grad_two_kernel, hid, p_og, (g_one, to_a), 2, [taps])
    total = keep + swap(send, "depth", 0)
    steps = [("depth", 1 << k) for k in range(1, lax.axis_size("depth").bit_length() - 1)]
    steps += [("space", 1 << k) for k in range(lax.axis_size("space").bit_length() - 1)]
    types = [BF if s[0] == "space" and s[1] > 1 else F32 for s in steps[1:]] + [F32]
    received = partner(total, *steps[0])
    output, token = second(mask, t2, hid, total, False, us=0.1)
    total = add_after(total, received, token, types[0])
    hid, pre = lay(lay_x_kernel, "lay_x", hid, pre, sa, sb, token)
    received = partner(total, *steps[1])
    output, token = second(mask, t2, hid, total, True, (output,))
    total = add_after(total, received, token, types[1])
    received = partner(total, *steps[2])
    grad_input, token = second(mask, t1b, pre, total, False)
    total = add_after(total, received, token, types[2])
    for step, kind in zip(steps[3:], types[3:]):
        total = add_after(total, partner(total, *step), token, kind)
    other = swap(total, "depth", 0)
    grad_input, _ = second(mask, t1b, pre, total, True, (grad_input,))
    grad_one, grad_two = finish(total, other, span)
    return output, grad_input, grad_one, grad_two


def solution(mesh):
    field = P(("groups", "space"), None, "depth", None)
    in_specs = (field, P(("groups", "space"), "depth", None), P(), P(), field)
    out_specs = (field, field, P("groups", None), P("groups", None))
    return jax.shard_map(shards, mesh=mesh, in_specs=in_specs, out_specs=out_specs, check_vma=False)
```

```python
import functools

import jax
import jax.numpy as jnp
from jax import lax
from jax.experimental import pallas as pl
from jax.experimental.pallas import tpu as pltpu
from jax.sharding import PartitionSpec as P

BRICK = 8
BX, BY = 2, 4
IX, IY = BX + 2, BY + 2
BF = jnp.bfloat16
F32 = jnp.float32
VMEM = pltpu.VMEM
ANY = pl.ANY
LIMIT = 28 << 20


CHUNK = 4


def cost(us):
    return pl.CostEstimate(flops=int(us * 1.1e9), bytes_accessed=1 << 20, transcendentals=0)


def lane_ids(shape):
    return lax.broadcasted_iota(jnp.int32, shape, len(shape) - 1)


HB = pl.BlockSpec(memory_space=ANY)
VM = pl.BlockSpec(memory_space=VMEM)
PARAMS = pltpu.CompilerParams(vmem_limit_bytes=LIMIT)


def is_odd(axis):
    return lax.rem(lax.axis_index(axis), 2) == 1


def by_parity(odd, low, high, ref_a, ref_b):
    @pl.when(odd)
    def _():
        ref_a(low)
        ref_b(high)

    @pl.when(jnp.logical_not(odd))
    def _():
        ref_a(high)
        ref_b(low)


def place(acc, piece, lane, at):
    shift = (at - lane) % 128
    if shift:
        piece = pltpu.roll(piece, shift, 1)
    here = lane_ids(piece.shape) // 32 == (at % 128) // 32
    acc[at // 128] = jnp.where(here, piece, acc[at // 128])


def lay_bands(w_ref, outs, which, interleave):
    width = 32
    lanes = lane_ids((width, 128))

    square = (BY * width, BY * width)
    row = lax.broadcasted_iota(jnp.int32, square, 0)
    perm = jnp.where(lane_ids(square) == (row % BY) * width + row // BY, 1.0, 0.0).astype(BF)

    def band(pick, out, interleave):
        base = [[jnp.zeros((width, 128), F32) for _ in range(6)] for _ in range(3)]
        for dx in range(3):
            for dy in range(3):
                for dz in range(3):
                    at = (dx * IY + dy) * width
                    piece, lane = pick((dx * 3 + dy) * 3 + dz)
                    place(base[dz], piece, lane, at)
        zero = jnp.zeros((width, 128), F32)
        for dz in range(3):
            turned = {0: base[dz]}
            for q in range(1, 4):
                rolled = [pltpu.roll(b, q * width, 1) for b in base[dz]]
                turned[q] = [
                    jnp.where(lanes < q * width, rolled[k - 1] if k else zero, rolled[k])
                    for k in range(6)
                ]
            for xo in range(BX):
                for k in range(6):
                    group = []
                    for yo in range(BY):
                        off = xo * IY + yo
                        moved, part = off // 4, off % 4
                        group.append(turned[part][k - moved] if k >= moved else zero)
                    group = jnp.concatenate(group, 0).astype(BF)
                    if interleave:
                        group = jnp.dot(perm, group, preferred_element_type=F32).astype(BF)
                    row = (dz * BX + xo) * BY * width
                    out[row : row + BY * width, k * 128 : (k + 1) * 128] = group

    def straight(which):
        def pick(tap):
            lane = tap * width
            col = lane // 128 * 128
            return w_ref[which, :, col : col + 128], lane % 128

        return pick

    def flipped(which):
        pad = jnp.zeros((128 - width, 896), F32)
        turned = jnp.concatenate([w_ref[which], pad], 0).T

        def pick(tap):
            back = 26 - tap
            return turned[back * width : (back + 1) * width], 0

        return pick

    band(straight(which), outs[0], interleave)
    band(flipped(1 - which), outs[1], interleave)


def grid_of(arr_shape):
    size_x, width, size_y, size_z = arr_shape
    return (size_x + 2, size_y + 2, width, size_z)


def relayout_kernel(occ, w1, w2, feat, cot, mask, t1, t2b, t2, t1b, p_in, p_og, *scratch):
    held, w_held, w_wide, occ_held, perm, sem, w_sem = scratch
    size_x, width, size_y = feat.shape[:3]
    n = width * size_y
    copies = [
        [
            pltpu.make_async_copy(
                src.at[pl.ds(x, CHUNK)], held.at[which, pl.ds(x, CHUNK)], sem.at[which, x // CHUNK]
            )
            for x in range(0, size_x, CHUNK)
        ]
        for which, src in enumerate((feat, cot))
    ]
    w_copies = [
        pltpu.make_async_copy(src, w_held.at[which], w_sem.at[which])
        for which, src in enumerate((w1, w2))
    ]
    occ_copy = pltpu.make_async_copy(occ, occ_held, w_sem.at[2])
    for c in w_copies + [occ_copy] + sum(copies, []):
        c.start()
    row = lax.broadcasted_iota(jnp.int32, (n, n), 0)
    at = (row % width) * size_y + row // width
    perm[...] = jnp.where(lane_ids((n, n)) == at, 1.0, 0.0).astype(BF)
    w_wide[...] = jnp.zeros_like(w_wide)
    for which, c in enumerate(w_copies):
        c.wait()
        w_wide[which, :, : w1.shape[1]] = w_held[which].astype(F32)
    lay_bands(w_wide, (t1, t2b), 0, False)
    lay_bands(w_wide, (t2, t1b), 1, True)
    occ_copy.wait()
    lanes = lane_ids((1, 128)) // BRICK
    for i in range(occ.shape[0]):
        for j in range(occ.shape[1]):
            row = jnp.zeros((1, 128), F32)
            for k in range(occ.shape[2]):
                row = jnp.where(lanes == k, occ_held[i, j, k].astype(F32), row)
            mask[i, j] = row
    for which, dst in enumerate((p_in, p_og)):
        for c in copies[which]:
            c.wait()
        for x in range(0, size_x, 2):
            wide = jnp.concatenate([held[which, x + k].reshape(n, 128) for k in range(2)], 1)
            moved = jnp.dot(perm[...], wide, preferred_element_type=F32)
            for k in range(2):
                for brick_y in range(size_y // BRICK):
                    y = slice(1 + brick_y * BRICK, 1 + (brick_y + 1) * BRICK)
                    value = moved[brick_y * BRICK * width : (brick_y + 1) * BRICK * width]
                    value = value[:, k * 128 : (k + 1) * 128] * mask[x // BRICK, brick_y]
                    dst[1 + x + k, y] = value.astype(BF).reshape(BRICK, width, 128)


def relayout(occ, w1, w2, feat, cot):
    size_x, width, size_y, size_z = feat.shape
    arr = jax.ShapeDtypeStruct(grid_of(feat.shape), BF)
    hbm = pl.BlockSpec(memory_space=pltpu.HBM)
    band = jax.ShapeDtypeStruct((3 * BX * BY * width, IX * IY * width), BF)
    return pl.pallas_call(
        relayout_kernel,
        in_specs=[hbm] * 5,
        out_specs=[VM] * 7,
        out_shape=[jax.ShapeDtypeStruct((*occ.shape[:2], 1, size_z), F32)] + [band] * 4 + [arr] * 2,
        scratch_shapes=[
            VMEM((2, *feat.shape), BF),
            VMEM((2, *w1.shape), BF),
            VMEM((2, 32, 896), F32),
            pltpu.SMEM(occ.shape, jnp.int32),
            VMEM((width * size_y, width * size_y), BF),
            pltpu.SemaphoreType.DMA((2, size_x // CHUNK)),
            pltpu.SemaphoreType.DMA((3,)),
        ],
        compiler_params=PARAMS,
        cost_estimate=pl.CostEstimate(flops=int(4e9), bytes_accessed=1 << 22, transcendentals=0),
        name="relayout",
    )(occ, w1, w2, feat, cot)


def y_rims_kernel(one, two, to_a, to_b):
    size_x, size_y = one.shape[0] - 2, one.shape[1] - 2

    def lay(ref):
        def put(y):
            for which, src in enumerate((one, two)):
                ref[which] = src[1 : size_x + 1, y]

        return put

    by_parity(is_odd("depth"), 1, size_y, lay(to_a), lay(to_b))


def x_rims_kernel(one, two, after, to_a, to_b):
    def lay(ref):
        def put(x):
            for which, src in enumerate((one, two)):
                ref[which] = src[x]

        return put

    by_parity(is_odd("space"), 1, one.shape[0] - 2, lay(to_a), lay(to_b))


def rims(kernel, name, length, one, two, *after):
    shape = jax.ShapeDtypeStruct((2, length, *one.shape[2:]), BF)
    return pl.pallas_call(
        kernel,
        in_specs=[VM] * (2 + len(after)),
        out_specs=[VM, VM],
        out_shape=[shape, shape],
        compiler_params=PARAMS,
        cost_estimate=cost(0.1),
        name=name,
    )(one, two, *after)


def lay_y_kernel(one, two, da, db, after, one_out, two_out):
    size_x, size_y = one.shape[0] - 2, one.shape[1] - 2
    spot = jnp.where(is_odd("depth"), 0, size_y + 1)
    for which, dst in enumerate((one_out, two_out)):
        dst[1 : size_x + 1, pl.ds(spot, 1)] = da[which][:, None]
        dst[1 : size_x + 1, pl.ds(size_y + 1 - spot, 1)] = db[which][:, None]


def lay_x_kernel(one, two, sa, sb, after, one_out, two_out):
    size_x = one.shape[0] - 2
    spot = jnp.where(is_odd("space"), 0, size_x + 1)
    for which, dst in enumerate((one_out, two_out)):
        dst[pl.ds(spot, 1)] = sa[which][None]
        dst[pl.ds(size_x + 1 - spot, 1)] = sb[which][None]


def lay(kernel, name, one, two, got_a, got_b, after):
    shape = jax.ShapeDtypeStruct(one.shape, BF)
    return pl.pallas_call(
        kernel,
        in_specs=[VM] * 5,
        out_specs=[VM, VM],
        out_shape=[shape, shape],
        input_output_aliases={0: 0, 1: 1},
        compiler_params=PARAMS,
        cost_estimate=cost(0.1),
        name=name,
    )(one, two, got_a, got_b, after)


def block_input(padded, bx, pair):
    parts = []
    for by in pair:
        part = padded[pl.ds(BX * bx, IX), BY * by : BY * by + IY]
        parts.append(part.reshape(IX * IY * 32, 128))
    return jnp.concatenate(parts, 1)


def z_sum(product, half):
    n = BX * BY * 32
    p = product[:, half * 128 : (half + 1) * 128]
    lanes = lane_ids((n, 128))
    below = jnp.where(lanes > 0, pltpu.roll(p[:n], 1, 1), 0.0)
    above = jnp.where(lanes < 127, pltpu.roll(p[2 * n :], 127, 1), 0.0)
    return p[n : 2 * n] + below + above


def first_kernel(mask, t_one, t_two, p_in, p_og, *rest, edge, pairs):
    hid, pre = rest[-2:]
    last = (hid.shape[0] - 2) // BX - 1
    bxs = (0, last) if edge else range(1, last)
    for bx in bxs:
        x = pl.ds(1 + bx * BX, BX)
        for pair in pairs:
            one = jnp.dot(t_one[...], block_input(p_in, bx, pair), preferred_element_type=F32)
            two = jnp.dot(t_two[...], block_input(p_og, bx, pair), preferred_element_type=F32)
            for half, by in enumerate(pair):
                m = mask[bx * BX // BRICK, by * BY // BRICK]
                act = z_sum(one, half)
                grad = z_sum(two, half)
                sig = 1.0 / (1.0 + jnp.exp(-act))
                hidden = (act * sig * m).astype(BF)
                slope = (grad * sig * (1.0 + act * (1.0 - sig)) * m).astype(BF)
                y = slice(1 + by * BY, 1 + (by + 1) * BY)
                hid[x, y] = hidden.reshape(BX, BY, 32, 128)
                pre[x, y] = slope.reshape(BX, BY, 32, 128)


def first(mask, t_one, t_two, p_in, p_og, onto, edge, pairs):
    arr = jax.ShapeDtypeStruct(p_in.shape, BF)
    return pl.pallas_call(
        functools.partial(first_kernel, edge=edge, pairs=pairs),
        in_specs=[VM] * (5 + len(onto)),
        out_specs=[VM] * 2,
        out_shape=[arr] * 2,
        input_output_aliases={5: 0, 6: 1} if onto else {},
        compiler_params=PARAMS,
        cost_estimate=cost(5),
        name="first",
    )(mask, t_one, t_two, p_in, p_og, *onto)


def second_kernel(mask, t, padded, after, *rest, bxs, span):
    if span:
        own, other = rest[:2]
        out_one, out_two, wide, g_sem = rest[-8], rest[-7], rest[-2], rest[-1]
        out, token, held, sem = rest[-6:-2]
        finish_grads(own, other, wide, span)
        g_copies = [
            pltpu.make_async_copy(wide.at[k], ref, g_sem.at[k])
            for k, ref in enumerate((out_one, out_two))
        ]
        for made in g_copies:
            made.start()
    else:
        g_copies = []
        out, token, held, sem = rest[-4:]
    width, size_y = out.shape[1], out.shape[2]
    token[...] = jnp.zeros_like(token)
    low_half = lax.broadcasted_iota(jnp.int32, (BX * width // 2, 8, 128), 1) < BY
    copies = []
    for slot, bx in enumerate(bxs):
        pairs = []
        for at in range(0, size_y // BY, 2):
            pair = (at, at + 1)
            product = jnp.dot(t[...], block_input(padded, bx, pair), preferred_element_type=F32)
            m = mask[bx * BX // BRICK, at * BY // BRICK]
            left, right = [(z_sum(product, h) * m).reshape(low_half.shape) for h in range(2)]
            even = jnp.where(low_half, left, pltpu.roll(right, BY, 1))
            odd = jnp.where(low_half, pltpu.roll(left, BY, 1), right)
            both = jnp.stack([even, odd], 1)
            pairs.append(both.reshape(BX, width, 8, 128))
        held[slot] = jnp.concatenate(pairs, 2).astype(BF)
        made = pltpu.make_async_copy(held.at[slot], out.at[pl.ds(bx * BX, BX)], sem.at[slot])
        made.start()
        copies.append(made)
    for made in copies + g_copies:
        made.wait()


def second(mask, t, padded, after, bxs, onto=(), us=4, grads=(), span=0):
    size_x, size_y, width, size_z = padded.shape
    size_x, size_y = size_x - 2, size_y - 2
    slots = len(bxs)
    grad = [jax.ShapeDtypeStruct((32, 27 * 32), F32)] * len(grads)
    more = [VMEM((2, 32, 27 * 32), F32), pltpu.SemaphoreType.DMA((2,))] if grads else []
    return pl.pallas_call(
        functools.partial(second_kernel, bxs=bxs, span=span),
        in_specs=[VM] * (4 + len(grads)) + [HB] * len(onto),
        out_specs=[HB] * len(grad) + [HB, VM],
        out_shape=grad
        + [
            jax.ShapeDtypeStruct((size_x, width, size_y, size_z), BF),
            jax.ShapeDtypeStruct((8, 128), F32),
        ],
        input_output_aliases={4 + len(grads): len(grad)} if onto else {},
        scratch_shapes=[
            VMEM((slots, BX, width, size_y, size_z), BF),
            pltpu.SemaphoreType.DMA((slots,)),
        ]
        + more,
        compiler_params=PARAMS,
        cost_estimate=cost(us),
        name="second",
    )(mask, t, padded, after, *grads, *onto)


def grad_sum(g, padded, total):
    size_y = g.shape[1] - 2
    n = BX * BY * 32
    lhs, rhs = [], []
    for bx in range((g.shape[0] - 2) // BX):
        for by in range(size_y // BY):
            x, y = pl.ds(1 + bx * BX, BX), slice(1 + by * BY, 1 + (by + 1) * BY)
            block = g[x, y].reshape(n, 128).astype(F32)
            lanes = lane_ids((n, 128))
            ahead = jnp.where(lanes < 127, pltpu.roll(block, 127, 1), 0.0)
            behind = jnp.where(lanes > 0, pltpu.roll(block, 1, 1), 0.0)
            lhs.append(jnp.concatenate([ahead, block, behind], 0).astype(BF))
        rhs += [block_input(padded, bx, (at, at + 1)) for at in range(0, size_y // BY, 2)]
    lhs, rhs = jnp.concatenate(lhs, 1), jnp.concatenate(rhs, 1)
    total[...] = lax.dot_general(lhs, rhs, (((1,), (1,)), ((), ())), preferred_element_type=F32)


def grad_taps(total, out):
    lanes = IX * IY * 32
    for dz in range(3):
        acc = jnp.zeros((32, lanes), F32)
        for xo in range(BX):
            for yo in range(BY):
                row = ((dz * BX + xo) * BY + yo) * 32
                part = total[row : row + 32, :]
                shift = (xo * IY + yo) * 32
                acc += pltpu.roll(part, lanes - shift, 1) if shift else part
        for dx in range(3):
            at = dx * IY * 32
            moved = pltpu.roll(acc, lanes - at, 1) if at else acc
            out[dx, dz * 32 : (dz + 1) * 32, :] = moved[:, :128]


def grad_one_kernel(g, padded, out, total):
    grad_sum(g, padded, total)
    grad_taps(total, out)


def grad_two_kernel(g, padded, one, after, keep, send, taps, total):
    grad_sum(g, padded, total)
    grad_taps(total, taps)

    def store(ref):
        def put(value):
            ref[...] = value

        return put

    by_parity(is_odd("depth"), taps[...], one[...], store(keep), store(send))


def kernel_grad(kernel, g, padded, extra=(), outs=1, scratch=()):
    taps = jax.ShapeDtypeStruct((3, 96, 128), F32)
    return pl.pallas_call(
        kernel,
        in_specs=[VM] * (2 + len(extra)),
        out_specs=[VM] * outs,
        out_shape=[taps] * outs,
        scratch_shapes=list(scratch) + [VMEM((3 * BX * BY * 32, IX * IY * 32), F32)],
        compiler_params=PARAMS,
        cost_estimate=cost(8),
        name="kernel_grad",
    )(g, padded, *extra)


def finish_grads(own, other, wide, span):
    def zeros():
        return [jnp.zeros((32, 128), F32) for _ in range(7)]

    def write(acc, out):
        for k in range(7):
            end = min((k + 1) * 128, wide.shape[2])
            wide[out, :, k * 128 : end] = acc[k][:, : end - k * 128] / span

    def both(one, two):
        acc = zeros()
        for dx in range(3):
            for dz in range(3):
                block = one[dx, dz * 32 : (dz + 1) * 32, :]
                for dy in range(3):
                    place(acc, block, dy * 32, ((dx * 3 + dy) * 3 + dz) * 32)
        write(acc, 0)
        acc = zeros()
        pad = jnp.zeros((96, 128), F32)
        for dx in range(3):
            for dz in range(3):
                block = two[dx, dz * 32 : (dz + 1) * 32, :]
                turned = jnp.concatenate([block, pad], 0).T
                for dy in range(3):
                    tap = ((2 - dx) * 3 + 2 - dy) * 3 + 2 - dz
                    place(acc, turned[dy * 32 : (dy + 1) * 32], 0, tap * 32)
        write(acc, 1)

    odd = is_odd("depth")

    @pl.when(odd)
    def _():
        both(other, own)

    @pl.when(jnp.logical_not(odd))
    def _():
        both(own, other)


def swap(x, axis, phase):
    n = lax.axis_size(axis)
    pairs = []
    for i in range(phase, n - 1, 2):
        pairs += [(i, i + 1), (i + 1, i)]
    return lax.ppermute(x, axis, pairs)


def both_phases(to_a, to_b, axis):
    return swap(to_a, axis, 0), swap(to_b, axis, 1)


def add_kernel(x, y, after, out):
    out[...] = (x[...].astype(F32) + y[...].astype(F32)).astype(out.dtype)


def add_after(x, y, after, dtype=F32):
    return pl.pallas_call(
        add_kernel,
        in_specs=[VM, VM, VM],
        out_specs=VM,
        out_shape=jax.ShapeDtypeStruct(x.shape, dtype),
        compiler_params=PARAMS,
        cost_estimate=cost(0.1),
        name="add_after",
    )(x, y, after)


def partner(x, axis, step):
    return lax.ppermute(x, axis, [(i, i ^ step) for i in range(lax.axis_size(axis))])


def shards(features, occupancy, weight_one, weight_two, cotangent):
    span = features.shape[0] * lax.axis_size("space")

    size_x, size_y = features.shape[0], features.shape[2]
    by = range(size_y // BY)
    middle, ends = [by[k : k + 2] for k in by[1:-1:2]], [(by[0], by[-1])]

    args = (occupancy, weight_one, weight_two, features, cotangent)
    in_hbm = [pltpu.with_memory_space_constraint(v, pltpu.HBM) for v in args]
    mask, t1, t2b, t2, t1b, p_in, p_og = relayout(*in_hbm)
    da, db = both_phases(*rims(y_rims_kernel, "y_rims", size_x, p_in, p_og), "depth")
    out = first(mask, t1, t2b, p_in, p_og, (), False, middle)
    p_in, p_og = lay(lay_y_kernel, "lay_y", p_in, p_og, da, db, out[0])
    to_a, to_b = rims(x_rims_kernel, "x_rims", size_y + 2, p_in, p_og, t2)
    sa, sb = both_phases(to_a, to_b, "space")
    out = first(mask, t1, t2b, p_in, p_og, out, False, ends)
    p_in, p_og = lay(lay_x_kernel, "lay_x", p_in, p_og, sa, sb, out[0])
    hid, pre = first(mask, t1, t2b, p_in, p_og, out, True, middle + ends)

    da, db = both_phases(*rims(y_rims_kernel, "y_rims", size_x, hid, pre), "depth")
    (g_one,) = kernel_grad(grad_one_kernel, pre, p_in)
    hid, pre = lay(lay_y_kernel, "lay_y", hid, pre, da, db, g_one)
    to_a, to_b = rims(x_rims_kernel, "x_rims", size_y + 2, hid, pre, g_one)
    sa, sb = both_phases(to_a, to_b, "space")
    taps = VMEM((3, 96, 128), F32)
    keep, send = kernel_grad(grad_two_kernel, hid, p_og, (g_one, to_a), 2, [taps])
    steps = [("depth", 1 << k) for k in range(1, lax.axis_size("depth").bit_length() - 1)]
    steps += [("space", 1 << k) for k in range(lax.axis_size("space").bit_length() - 1)]
    types = [BF] * 3 + [F32] * (len(steps) - 2)
    total = add_after(keep, swap(send, "depth", 0), keep, types[0])
    n = size_x // BX
    inner, low, high = tuple(range(2, n - 2)), (0, 1), (n - 2, n - 1)
    received = partner(total, *steps[0])
    output, token = second(mask, t2, hid, total, inner)
    total = add_after(total, received, token, types[1])
    received = partner(total, *steps[1])
    grad_input, token = second(mask, t1b, pre, total, inner)
    total = add_after(total, received, token, types[2])
    hid, pre = lay(lay_x_kernel, "lay_x", hid, pre, sa, sb, token)
    received = partner(total, *steps[2])
    output, token = second(mask, t2, hid, total, low + high, (output,))
    total = add_after(total, received, token, types[3])
    for step, kind in zip(steps[3:], types[4:]):
        total = add_after(total, partner(total, *step), token, kind)
    other = swap(total, "depth", 0)
    grad_input, token = second(mask, t1b, pre, total, low, (grad_input,), us=2)
    grad_one, grad_two, grad_input, _ = second(
        mask, t1b, pre, token, high, (grad_input,), 3, (total, other), span
    )
    return output, grad_input, grad_one, grad_two


def solution(mesh):
    field = P(("groups", "space"), None, "depth", None)
    in_specs = (field, P(("groups", "space"), "depth", None), P(), P(), field)
    out_specs = (field, field, P("groups", None), P("groups", None))
    return jax.shard_map(shards, mesh=mesh, in_specs=in_specs, out_specs=out_specs, check_vma=False)
```

```python
import functools

import jax
import jax.numpy as jnp
from jax import lax
from jax.experimental import pallas as pl
from jax.experimental.pallas import tpu as pltpu
from jax.sharding import PartitionSpec as P

BRICK = 8
BX, BY = 2, 4
IX, IY = BX + 2, BY + 2
BF = jnp.bfloat16
F32 = jnp.float32
VMEM = pltpu.VMEM
ANY = pl.ANY
LIMIT = 28 << 20


CHUNK = 4


def cost(us):
    return pl.CostEstimate(flops=int(us * 1.1e9), bytes_accessed=1 << 20, transcendentals=0)


def lane_ids(shape):
    return lax.broadcasted_iota(jnp.int32, shape, len(shape) - 1)


HB = pl.BlockSpec(memory_space=ANY)
VM = pl.BlockSpec(memory_space=VMEM)
PARAMS = pltpu.CompilerParams(vmem_limit_bytes=LIMIT)


def is_odd(axis):
    return lax.rem(lax.axis_index(axis), 2) == 1


def by_parity(odd, low, high, ref_a, ref_b):
    @pl.when(odd)
    def _():
        ref_a(low)
        ref_b(high)

    @pl.when(jnp.logical_not(odd))
    def _():
        ref_a(high)
        ref_b(low)


def place(acc, piece, lane, at):
    shift = (at - lane) % 128
    if shift:
        piece = pltpu.roll(piece, shift, 1)
    here = lane_ids(piece.shape) // 32 == (at % 128) // 32
    acc[at // 128] = jnp.where(here, piece, acc[at // 128])


def lay_bands(w_ref, outs, which, interleave):
    width = 32
    lanes = lane_ids((width, 128))

    square = (BY * width, BY * width)
    row = lax.broadcasted_iota(jnp.int32, square, 0)
    perm = jnp.where(lane_ids(square) == (row % BY) * width + row // BY, 1.0, 0.0).astype(BF)

    def band(pick, out, interleave):
        base = [[jnp.zeros((width, 128), F32) for _ in range(6)] for _ in range(3)]
        for dx in range(3):
            for dy in range(3):
                for dz in range(3):
                    at = (dx * IY + dy) * width
                    piece, lane = pick((dx * 3 + dy) * 3 + dz)
                    place(base[dz], piece, lane, at)
        zero = jnp.zeros((width, 128), F32)
        for dz in range(3):
            turned = {0: base[dz]}
            for q in range(1, 4):
                rolled = [pltpu.roll(b, q * width, 1) for b in base[dz]]
                turned[q] = [
                    jnp.where(lanes < q * width, rolled[k - 1] if k else zero, rolled[k])
                    for k in range(6)
                ]
            for xo in range(BX):
                for k in range(6):
                    group = []
                    for yo in range(BY):
                        off = xo * IY + yo
                        moved, part = off // 4, off % 4
                        group.append(turned[part][k - moved] if k >= moved else zero)
                    group = jnp.concatenate(group, 0).astype(BF)
                    if interleave:
                        group = jnp.dot(perm, group, preferred_element_type=F32).astype(BF)
                    row = (dz * BX + xo) * BY * width
                    out[row : row + BY * width, k * 128 : (k + 1) * 128] = group

    def straight(which):
        def pick(tap):
            lane = tap * width
            col = lane // 128 * 128
            return w_ref[which, :, col : col + 128], lane % 128

        return pick

    def flipped(which):
        pad = jnp.zeros((128 - width, 896), F32)
        turned = jnp.concatenate([w_ref[which], pad], 0).T

        def pick(tap):
            back = 26 - tap
            return turned[back * width : (back + 1) * width], 0

        return pick

    band(straight(which), outs[0], interleave)
    band(flipped(1 - which), outs[1], interleave)


def grid_of(arr_shape):
    size_x, width, size_y, size_z = arr_shape
    return (size_x + 2, size_y + 2, width, size_z)


def relayout_kernel(occ, w1, w2, feat, cot, mask, t1, t2b, t2, t1b, p_in, p_og, *scratch):
    held, w_held, w_wide, occ_held, perm, sem, w_sem = scratch
    size_x, width, size_y = feat.shape[:3]
    n = width * size_y
    copies = [
        [
            pltpu.make_async_copy(
                src.at[pl.ds(x, CHUNK)], held.at[which, pl.ds(x, CHUNK)], sem.at[which, x // CHUNK]
            )
            for x in range(0, size_x, CHUNK)
        ]
        for which, src in enumerate((feat, cot))
    ]
    w_copies = [
        pltpu.make_async_copy(src, w_held.at[which], w_sem.at[which])
        for which, src in enumerate((w1, w2))
    ]
    occ_copy = pltpu.make_async_copy(occ, occ_held, w_sem.at[2])
    for c in w_copies + [occ_copy] + sum(copies, []):
        c.start()
    row = lax.broadcasted_iota(jnp.int32, (n, n), 0)
    at = (row % width) * size_y + row // width
    perm[...] = jnp.where(lane_ids((n, n)) == at, 1.0, 0.0).astype(BF)
    w_wide[...] = jnp.zeros_like(w_wide)
    for which, c in enumerate(w_copies):
        c.wait()
        w_wide[which, :, : w1.shape[1]] = w_held[which].astype(F32)
    lay_bands(w_wide, (t1, t2b), 0, False)
    occ_copy.wait()
    lanes = lane_ids((1, 128)) // BRICK
    for i in range(occ.shape[0]):
        for j in range(occ.shape[1]):
            row = jnp.zeros((1, 128), F32)
            for k in range(occ.shape[2]):
                row = jnp.where(lanes == k, occ_held[i, j, k].astype(F32), row)
            mask[i, j] = row
    for which, dst in enumerate((p_in, p_og)):
        for c in copies[which]:
            c.wait()
        for x in range(0, size_x, 2):
            wide = jnp.concatenate([held[which, x + k].reshape(n, 128) for k in range(2)], 1)
            moved = jnp.dot(perm[...], wide, preferred_element_type=F32)
            for k in range(2):
                for brick_y in range(size_y // BRICK):
                    y = slice(1 + brick_y * BRICK, 1 + (brick_y + 1) * BRICK)
                    value = moved[brick_y * BRICK * width : (brick_y + 1) * BRICK * width]
                    value = value[:, k * 128 : (k + 1) * 128] * mask[x // BRICK, brick_y]
                    dst[1 + x + k, y] = value.astype(BF).reshape(BRICK, width, 128)
        if which == 0:
            lay_bands(w_wide, (t2, t1b), 1, True)


def relayout(occ, w1, w2, feat, cot):
    size_x, width, size_y, size_z = feat.shape
    arr = jax.ShapeDtypeStruct(grid_of(feat.shape), BF)
    hbm = pl.BlockSpec(memory_space=pltpu.HBM)
    band = jax.ShapeDtypeStruct((3 * BX * BY * width, IX * IY * width), BF)
    return pl.pallas_call(
        relayout_kernel,
        in_specs=[hbm] * 5,
        out_specs=[VM] * 7,
        out_shape=[jax.ShapeDtypeStruct((*occ.shape[:2], 1, size_z), F32)] + [band] * 4 + [arr] * 2,
        scratch_shapes=[
            VMEM((2, *feat.shape), BF),
            VMEM((2, *w1.shape), BF),
            VMEM((2, 32, 896), F32),
            pltpu.SMEM(occ.shape, jnp.int32),
            VMEM((width * size_y, width * size_y), BF),
            pltpu.SemaphoreType.DMA((2, size_x // CHUNK)),
            pltpu.SemaphoreType.DMA((3,)),
        ],
        compiler_params=PARAMS,
        cost_estimate=pl.CostEstimate(flops=int(4e9), bytes_accessed=1 << 22, transcendentals=0),
        name="relayout",
    )(occ, w1, w2, feat, cot)


def y_rims_kernel(one, two, to_a, to_b):
    size_x, size_y = one.shape[0] - 2, one.shape[1] - 2

    def lay(ref):
        def put(y):
            for which, src in enumerate((one, two)):
                ref[which] = src[1 : size_x + 1, y]

        return put

    by_parity(is_odd("depth"), 1, size_y, lay(to_a), lay(to_b))


def x_rims_kernel(one, two, after, to_a, to_b):
    def lay(ref):
        def put(x):
            for which, src in enumerate((one, two)):
                ref[which] = src[x]

        return put

    by_parity(is_odd("space"), 1, one.shape[0] - 2, lay(to_a), lay(to_b))


def rims(kernel, name, length, one, two, *after):
    shape = jax.ShapeDtypeStruct((2, length, *one.shape[2:]), BF)
    return pl.pallas_call(
        kernel,
        in_specs=[VM] * (2 + len(after)),
        out_specs=[VM, VM],
        out_shape=[shape, shape],
        compiler_params=PARAMS,
        cost_estimate=cost(0.1),
        name=name,
    )(one, two, *after)


def lay_y_kernel(one, two, da, db, after, one_out, two_out):
    size_x, size_y = one.shape[0] - 2, one.shape[1] - 2
    spot = jnp.where(is_odd("depth"), 0, size_y + 1)
    for which, dst in enumerate((one_out, two_out)):
        dst[1 : size_x + 1, pl.ds(spot, 1)] = da[which][:, None]
        dst[1 : size_x + 1, pl.ds(size_y + 1 - spot, 1)] = db[which][:, None]


def lay_x_kernel(one, two, sa, sb, after, one_out, two_out):
    size_x = one.shape[0] - 2
    spot = jnp.where(is_odd("space"), 0, size_x + 1)
    for which, dst in enumerate((one_out, two_out)):
        dst[pl.ds(spot, 1)] = sa[which][None]
        dst[pl.ds(size_x + 1 - spot, 1)] = sb[which][None]


def lay(kernel, name, one, two, got_a, got_b, after):
    shape = jax.ShapeDtypeStruct(one.shape, BF)
    return pl.pallas_call(
        kernel,
        in_specs=[VM] * 5,
        out_specs=[VM, VM],
        out_shape=[shape, shape],
        input_output_aliases={0: 0, 1: 1},
        compiler_params=PARAMS,
        cost_estimate=cost(0.1),
        name=name,
    )(one, two, got_a, got_b, after)


def block_input(padded, bx, pair):
    parts = []
    for by in pair:
        part = padded[pl.ds(BX * bx, IX), BY * by : BY * by + IY]
        parts.append(part.reshape(IX * IY * 32, 128))
    return jnp.concatenate(parts, 1)


def z_sum(product, half):
    n = BX * BY * 32
    p = product[:, half * 128 : (half + 1) * 128]
    lanes = lane_ids((n, 128))
    below = jnp.where(lanes > 0, pltpu.roll(p[:n], 1, 1), 0.0)
    above = jnp.where(lanes < 127, pltpu.roll(p[2 * n :], 127, 1), 0.0)
    return p[n : 2 * n] + below + above


def first_kernel(mask, t_one, t_two, p_in, p_og, *rest, edge, pairs):
    hid, pre = rest[-2:]
    last = (hid.shape[0] - 2) // BX - 1
    bxs = (0, last) if edge else range(1, last)
    for bx in bxs:
        x = pl.ds(1 + bx * BX, BX)
        for pair in pairs:
            one = jnp.dot(t_one[...], block_input(p_in, bx, pair), preferred_element_type=F32)
            two = jnp.dot(t_two[...], block_input(p_og, bx, pair), preferred_element_type=F32)
            for half, by in enumerate(pair):
                m = mask[bx * BX // BRICK, by * BY // BRICK]
                act = z_sum(one, half)
                grad = z_sum(two, half)
                sig = 1.0 / (1.0 + jnp.exp(-act))
                hidden = (act * sig * m).astype(BF)
                slope = (grad * sig * (1.0 + act * (1.0 - sig)) * m).astype(BF)
                y = slice(1 + by * BY, 1 + (by + 1) * BY)
                hid[x, y] = hidden.reshape(BX, BY, 32, 128)
                pre[x, y] = slope.reshape(BX, BY, 32, 128)


def first(mask, t_one, t_two, p_in, p_og, onto, edge, pairs):
    arr = jax.ShapeDtypeStruct(p_in.shape, BF)
    return pl.pallas_call(
        functools.partial(first_kernel, edge=edge, pairs=pairs),
        in_specs=[VM] * (5 + len(onto)),
        out_specs=[VM] * 2,
        out_shape=[arr] * 2,
        input_output_aliases={5: 0, 6: 1} if onto else {},
        compiler_params=PARAMS,
        cost_estimate=cost(5),
        name="first",
    )(mask, t_one, t_two, p_in, p_og, *onto)


def copies_out(held, out, bxs, sem):
    return [
        pltpu.make_async_copy(held.at[slot], out.at[pl.ds(bx * BX, BX)], sem.at[slot])
        for slot, bx in enumerate(bxs)
    ]


def second_kernel(mask, t, padded, after, *rest, bxs, prev_bxs, final, span, n_in):
    ins, rest = list(rest[:n_in]), list(rest[n_in:])
    copies = []
    if span:
        own, other = ins[:2]
        g_outs = [rest.pop(0), rest.pop(0)]
    if prev_bxs:
        out = rest.pop(0)
        prev, prev_sem = ins[2 if span else 0], rest.pop()
        copies += copies_out(prev, out, prev_bxs, prev_sem)
        for made in copies:
            made.start()
    if span:
        g_sem, wide = rest.pop(), rest.pop()
        finish_grads(own, other, wide, span)
        for k, ref in enumerate(g_outs):
            made = pltpu.make_async_copy(wide.at[k], ref, g_sem.at[k])
            made.start()
            copies.append(made)
    held = rest.pop(0)
    width, size_y = held.shape[2], held.shape[3]
    last_copies = copies_out(held, out, bxs, rest.pop()) if final else []
    low_half = lax.broadcasted_iota(jnp.int32, (BX * width // 2, 8, 128), 1) < BY
    for slot, bx in enumerate(bxs):
        pairs = []
        for at in range(0, size_y // BY, 2):
            pair = (at, at + 1)
            product = jnp.dot(t[...], block_input(padded, bx, pair), preferred_element_type=F32)
            m = mask[bx * BX // BRICK, at * BY // BRICK]
            left, right = [(z_sum(product, h) * m).reshape(low_half.shape) for h in range(2)]
            even = jnp.where(low_half, left, pltpu.roll(right, BY, 1))
            odd = jnp.where(low_half, pltpu.roll(left, BY, 1), right)
            both = jnp.stack([even, odd], 1)
            pairs.append(both.reshape(BX, width, 8, 128))
        held[slot] = jnp.concatenate(pairs, 2).astype(BF)
        if final:
            last_copies[slot].start()
    for made in copies + last_copies:
        made.wait()


def second(mask, t, padded, after, bxs, prev=None, grads=(), span=0, final=False, us=4):
    size_x, size_y, width, size_z = padded.shape
    size_x, size_y = size_x - 2, size_y - 2
    held = (len(bxs), BX, width, size_y, size_z)
    prev_held, prev_bxs, onto = prev or (None, (), None)
    extra = list(grads) + ([prev_held] if prev else []) + ([] if onto is None else [onto])
    outs = [jax.ShapeDtypeStruct((32, 27 * 32), F32)] * len(grads)
    if prev:
        outs.append(jax.ShapeDtypeStruct((size_x, width, size_y, size_z), BF))
    specs = [HB] * len(outs)
    scratch = []
    if final:
        scratch.append(VMEM(held, BF))
        scratch.append(pltpu.SemaphoreType.DMA((len(bxs),)))
    else:
        outs.append(jax.ShapeDtypeStruct(held, BF))
        specs.append(VM)
    if grads:
        scratch += [VMEM((2, 32, 27 * 32), F32), pltpu.SemaphoreType.DMA((2,))]
    if prev:
        scratch.append(pltpu.SemaphoreType.DMA((len(prev_bxs),)))
    n_in = len(extra)
    in_specs = [VM] * (4 + n_in - (onto is not None)) + [HB] * (onto is not None)
    return pl.pallas_call(
        functools.partial(
            second_kernel, bxs=bxs, prev_bxs=prev_bxs, final=final, span=span, n_in=n_in
        ),
        in_specs=in_specs,
        out_specs=specs,
        out_shape=outs,
        input_output_aliases={} if onto is None else {3 + n_in: len(grads)},
        scratch_shapes=scratch,
        compiler_params=PARAMS,
        cost_estimate=cost(us),
        name="second",
    )(mask, t, padded, after, *extra)


def grad_sum(g, padded, total):
    size_y = g.shape[1] - 2
    n = BX * BY * 32
    lhs, rhs = [], []
    for bx in range((g.shape[0] - 2) // BX):
        for by in range(size_y // BY):
            x, y = pl.ds(1 + bx * BX, BX), slice(1 + by * BY, 1 + (by + 1) * BY)
            block = g[x, y].reshape(n, 128).astype(F32)
            lanes = lane_ids((n, 128))
            ahead = jnp.where(lanes < 127, pltpu.roll(block, 127, 1), 0.0)
            behind = jnp.where(lanes > 0, pltpu.roll(block, 1, 1), 0.0)
            lhs.append(jnp.concatenate([ahead, block, behind], 0).astype(BF))
        rhs += [block_input(padded, bx, (at, at + 1)) for at in range(0, size_y // BY, 2)]
    lhs, rhs = jnp.concatenate(lhs, 1), jnp.concatenate(rhs, 1)
    total[...] = lax.dot_general(lhs, rhs, (((1,), (1,)), ((), ())), preferred_element_type=F32)


def grad_taps(total, out):
    lanes = IX * IY * 32
    for dz in range(3):
        acc = jnp.zeros((32, lanes), F32)
        for xo in range(BX):
            for yo in range(BY):
                row = ((dz * BX + xo) * BY + yo) * 32
                part = total[row : row + 32, :]
                shift = (xo * IY + yo) * 32
                acc += pltpu.roll(part, lanes - shift, 1) if shift else part
        for dx in range(3):
            at = dx * IY * 32
            moved = pltpu.roll(acc, lanes - at, 1) if at else acc
            out[dx, dz * 32 : (dz + 1) * 32, :] = moved[:, :128]


def grad_one_kernel(g, padded, out, total):
    grad_sum(g, padded, total)
    grad_taps(total, out)


def grad_two_kernel(g, padded, one, after, keep, send, taps, total):
    grad_sum(g, padded, total)
    grad_taps(total, taps)

    def store(ref):
        def put(value):
            ref[...] = value

        return put

    by_parity(is_odd("depth"), taps[...], one[...], store(keep), store(send))


def kernel_grad(kernel, g, padded, extra=(), outs=1, scratch=()):
    taps = jax.ShapeDtypeStruct((3, 96, 128), F32)
    return pl.pallas_call(
        kernel,
        in_specs=[VM] * (2 + len(extra)),
        out_specs=[VM] * outs,
        out_shape=[taps] * outs,
        scratch_shapes=list(scratch) + [VMEM((3 * BX * BY * 32, IX * IY * 32), F32)],
        compiler_params=PARAMS,
        cost_estimate=cost(8),
        name="kernel_grad",
    )(g, padded, *extra)


def finish_grads(own, other, wide, span):
    def zeros():
        return [jnp.zeros((32, 128), F32) for _ in range(7)]

    def write(acc, out):
        for k in range(7):
            end = min((k + 1) * 128, wide.shape[2])
            wide[out, :, k * 128 : end] = acc[k][:, : end - k * 128] / span

    def both(one, two):
        acc = zeros()
        for dx in range(3):
            for dz in range(3):
                block = one[dx, dz * 32 : (dz + 1) * 32, :]
                for dy in range(3):
                    place(acc, block, dy * 32, ((dx * 3 + dy) * 3 + dz) * 32)
        write(acc, 0)
        acc = zeros()
        pad = jnp.zeros((96, 128), F32)
        for dx in range(3):
            for dz in range(3):
                block = two[dx, dz * 32 : (dz + 1) * 32, :]
                turned = jnp.concatenate([block, pad], 0).T
                for dy in range(3):
                    tap = ((2 - dx) * 3 + 2 - dy) * 3 + 2 - dz
                    place(acc, turned[dy * 32 : (dy + 1) * 32], 0, tap * 32)
        write(acc, 1)

    odd = is_odd("depth")

    @pl.when(odd)
    def _():
        both(other, own)

    @pl.when(jnp.logical_not(odd))
    def _():
        both(own, other)


def swap(x, axis, phase):
    n = lax.axis_size(axis)
    pairs = []
    for i in range(phase, n - 1, 2):
        pairs += [(i, i + 1), (i + 1, i)]
    return lax.ppermute(x, axis, pairs)


def both_phases(to_a, to_b, axis):
    return swap(to_a, axis, 0), swap(to_b, axis, 1)


def add_kernel(x, y, after, out):
    out[...] = (x[...].astype(F32) + y[...].astype(F32)).astype(out.dtype)


def add_after(x, y, after, dtype=F32):
    return pl.pallas_call(
        add_kernel,
        in_specs=[VM, VM, VM],
        out_specs=VM,
        out_shape=jax.ShapeDtypeStruct(x.shape, dtype),
        compiler_params=PARAMS,
        cost_estimate=cost(0.1),
        name="add_after",
    )(x, y, after)


def partner(x, axis, step):
    return lax.ppermute(x, axis, [(i, i ^ step) for i in range(lax.axis_size(axis))])


def shards(features, occupancy, weight_one, weight_two, cotangent):
    span = features.shape[0] * lax.axis_size("space")

    size_x, size_y = features.shape[0], features.shape[2]
    by = range(size_y // BY)
    middle, ends = [by[k : k + 2] for k in by[1:-1:2]], [(by[0], by[-1])]

    args = (occupancy, weight_one, weight_two, features, cotangent)
    in_hbm = [pltpu.with_memory_space_constraint(v, pltpu.HBM) for v in args]
    mask, t1, t2b, t2, t1b, p_in, p_og = relayout(*in_hbm)
    da, db = both_phases(*rims(y_rims_kernel, "y_rims", size_x, p_in, p_og), "depth")
    out = first(mask, t1, t2b, p_in, p_og, (), False, middle)
    p_in, p_og = lay(lay_y_kernel, "lay_y", p_in, p_og, da, db, out[0])
    to_a, to_b = rims(x_rims_kernel, "x_rims", size_y + 2, p_in, p_og, t2)
    sa, sb = both_phases(to_a, to_b, "space")
    out = first(mask, t1, t2b, p_in, p_og, out, False, ends)
    p_in, p_og = lay(lay_x_kernel, "lay_x", p_in, p_og, sa, sb, out[0])
    hid, pre = first(mask, t1, t2b, p_in, p_og, out, True, middle + ends)

    da, db = both_phases(*rims(y_rims_kernel, "y_rims", size_x, hid, pre), "depth")
    (g_one,) = kernel_grad(grad_one_kernel, pre, p_in)
    hid, pre = lay(lay_y_kernel, "lay_y", hid, pre, da, db, g_one)
    to_a, to_b = rims(x_rims_kernel, "x_rims", size_y + 2, hid, pre, g_one)
    sa, sb = both_phases(to_a, to_b, "space")
    taps = VMEM((3, 96, 128), F32)
    keep, send = kernel_grad(grad_two_kernel, hid, p_og, (g_one, to_a), 2, [taps])
    steps = [("depth", 1 << k) for k in range(1, lax.axis_size("depth").bit_length() - 1)]
    steps += [("space", 1 << k) for k in range(lax.axis_size("space").bit_length() - 1)]
    types = [BF] * 3 + [F32] * (len(steps) - 2)
    total = add_after(keep, swap(send, "depth", 0), keep, types[0])
    n = size_x // BX
    inner, low, high = tuple(range(2, n - 2)), (0, 1), (n - 2, n - 1)
    received = partner(total, *steps[0])
    (held_a,) = second(mask, t2, hid, total, inner)
    total = add_after(total, received, held_a, types[1])
    received = partner(total, *steps[1])
    output, held_b = second(mask, t1b, pre, total, inner, (held_a, inner, None))
    total = add_after(total, received, held_b, types[2])
    hid, pre = lay(lay_x_kernel, "lay_x", hid, pre, sa, sb, held_b)
    received = partner(total, *steps[2])
    edges = low + high
    grad_input, held_c = second(mask, t2, hid, total, edges, (held_b, inner, None))
    total = add_after(total, received, held_c, types[3])
    for step, kind in zip(steps[3:], types[4:]):
        total = add_after(total, partner(total, *step), held_c, kind)
    other = swap(total, "depth", 0)
    output, held_d = second(mask, t1b, pre, total, low, (held_c, edges, output), us=2)
    grad_one, grad_two, grad_input = second(
        mask, t1b, pre, held_d, high, (held_d, low, grad_input), (total, other), span, True, us=3
    )
    return output, grad_input, grad_one, grad_two


def solution(mesh):
    field = P(("groups", "space"), None, "depth", None)
    in_specs = (field, P(("groups", "space"), "depth", None), P(), P(), field)
    out_specs = (field, field, P("groups", None), P("groups", None))
    return jax.shard_map(shards, mesh=mesh, in_specs=in_specs, out_specs=out_specs, check_vma=False)
```

```python
import functools

import jax
import jax.numpy as jnp
from jax import lax
from jax.experimental import pallas as pl
from jax.experimental.pallas import tpu as pltpu
from jax.sharding import PartitionSpec as P

BRICK = 8
BX, BY = 2, 2
IX, IY = BX + 2, BY + 2
BF = jnp.bfloat16
F32 = jnp.float32
VMEM = pltpu.VMEM
ANY = pl.ANY
LIMIT = 34 << 20


CHUNK = 4


def cost(us):
    return pl.CostEstimate(flops=int(us * 1.1e9), bytes_accessed=1 << 20, transcendentals=0)


def lane_ids(shape):
    return lax.broadcasted_iota(jnp.int32, shape, len(shape) - 1)


HB = pl.BlockSpec(memory_space=ANY)
VM = pl.BlockSpec(memory_space=VMEM)
PARAMS = pltpu.CompilerParams(vmem_limit_bytes=LIMIT)


def is_odd(axis):
    return lax.rem(lax.axis_index(axis), 2) == 1


def by_parity(odd, low, high, ref_a, ref_b):
    @pl.when(odd)
    def _():
        ref_a(low)
        ref_b(high)

    @pl.when(jnp.logical_not(odd))
    def _():
        ref_a(high)
        ref_b(low)


def place(acc, piece, lane, at):
    shift = (at - lane) % 128
    if shift:
        piece = pltpu.roll(piece, shift, 1)
    here = lane_ids(piece.shape) // 32 == (at % 128) // 32
    acc[at // 128] = jnp.where(here, piece, acc[at // 128])


def lay_bands(w_ref, outs, which, interleave):
    width = 32
    lanes = lane_ids((width, 128))

    square = (BY * width, BY * width)
    row = lax.broadcasted_iota(jnp.int32, square, 0)
    perm = jnp.where(lane_ids(square) == (row % BY) * width + row // BY, 1.0, 0.0).astype(BF)

    def band(pick, out, interleave):
        base = [[jnp.zeros((width, 128), F32) for _ in range(4)] for _ in range(3)]
        for dx in range(3):
            for dy in range(3):
                for dz in range(3):
                    at = (dx * IY + dy) * width
                    piece, lane = pick((dx * 3 + dy) * 3 + dz)
                    place(base[dz], piece, lane, at)
        zero = jnp.zeros((width, 128), F32)
        for dz in range(3):
            turned = {0: base[dz]}
            for q in range(1, 4):
                rolled = [pltpu.roll(b, q * width, 1) for b in base[dz]]
                turned[q] = [
                    jnp.where(lanes < q * width, rolled[k - 1] if k else zero, rolled[k])
                    for k in range(4)
                ]
            for xo in range(BX):
                for k in range(4):
                    group = []
                    for yo in range(BY):
                        off = xo * IY + yo
                        moved, part = off // 4, off % 4
                        group.append(turned[part][k - moved] if k >= moved else zero)
                    group = jnp.concatenate(group, 0).astype(BF)
                    if interleave:
                        group = jnp.dot(perm, group, preferred_element_type=F32).astype(BF)
                    row = (dz * BX + xo) * BY * width
                    out[row : row + BY * width, k * 128 : (k + 1) * 128] = group

    def straight(which):
        def pick(tap):
            lane = tap * width
            col = lane // 128 * 128
            return w_ref[which, :, col : col + 128], lane % 128

        return pick

    def flipped(which):
        pad = jnp.zeros((128 - width, 896), F32)
        turned = jnp.concatenate([w_ref[which], pad], 0).T

        def pick(tap):
            back = 26 - tap
            return turned[back * width : (back + 1) * width], 0

        return pick

    band(straight(which), outs[0], interleave)
    band(flipped(1 - which), outs[1], interleave)


def grid_of(arr_shape):
    size_x, width, size_y, size_z = arr_shape
    return (size_x + 2, size_y + 2, width, size_z)


def relayout_kernel(occ, w1, w2, feat, cot, mask, t1, t2b, t2, t1b, p_in, p_og, *scratch):
    held, w_held, w_wide, occ_held, perm, sem, w_sem = scratch
    size_x, width, size_y = feat.shape[:3]
    n = width * size_y
    copies = [
        [
            pltpu.make_async_copy(
                src.at[pl.ds(x, CHUNK)], held.at[which, pl.ds(x, CHUNK)], sem.at[which, x // CHUNK]
            )
            for x in range(0, size_x, CHUNK)
        ]
        for which, src in enumerate((feat, cot))
    ]
    w_copies = [
        pltpu.make_async_copy(src, w_held.at[which], w_sem.at[which])
        for which, src in enumerate((w1, w2))
    ]
    occ_copy = pltpu.make_async_copy(occ, occ_held, w_sem.at[2])
    for c in w_copies + [occ_copy] + sum(copies, []):
        c.start()
    row = lax.broadcasted_iota(jnp.int32, (n, n), 0)
    at = (row % width) * size_y + row // width
    perm[...] = jnp.where(lane_ids((n, n)) == at, 1.0, 0.0).astype(BF)
    w_wide[...] = jnp.zeros_like(w_wide)
    for which, c in enumerate(w_copies):
        c.wait()
        w_wide[which, :, : w1.shape[1]] = w_held[which].astype(F32)
    lay_bands(w_wide, (t1, t2b), 0, False)
    occ_copy.wait()
    lanes = lane_ids((1, 128)) // BRICK
    for i in range(occ.shape[0]):
        for j in range(occ.shape[1]):
            row = jnp.zeros((1, 128), F32)
            for k in range(occ.shape[2]):
                row = jnp.where(lanes == k, occ_held[i, j, k].astype(F32), row)
            mask[i, j] = row
    for which, dst in enumerate((p_in, p_og)):
        for c in copies[which]:
            c.wait()
        for x in range(0, size_x, 2):
            wide = jnp.concatenate([held[which, x + k].reshape(n, 128) for k in range(2)], 1)
            moved = jnp.dot(perm[...], wide, preferred_element_type=F32)
            for k in range(2):
                for brick_y in range(size_y // BRICK):
                    y = slice(1 + brick_y * BRICK, 1 + (brick_y + 1) * BRICK)
                    value = moved[brick_y * BRICK * width : (brick_y + 1) * BRICK * width]
                    value = value[:, k * 128 : (k + 1) * 128] * mask[x // BRICK, brick_y]
                    dst[1 + x + k, y] = value.astype(BF).reshape(BRICK, width, 128)
        if which == 0:
            lay_bands(w_wide, (t2, t1b), 1, True)


def relayout(occ, w1, w2, feat, cot):
    size_x, width, size_y, size_z = feat.shape
    arr = jax.ShapeDtypeStruct(grid_of(feat.shape), BF)
    hbm = pl.BlockSpec(memory_space=pltpu.HBM)
    band = jax.ShapeDtypeStruct((3 * BX * BY * width, IX * IY * width), BF)
    return pl.pallas_call(
        relayout_kernel,
        in_specs=[hbm] * 5,
        out_specs=[VM] * 7,
        out_shape=[jax.ShapeDtypeStruct((*occ.shape[:2], 1, size_z), F32)] + [band] * 4 + [arr] * 2,
        scratch_shapes=[
            VMEM((2, *feat.shape), BF),
            VMEM((2, *w1.shape), BF),
            VMEM((2, 32, 896), F32),
            pltpu.SMEM(occ.shape, jnp.int32),
            VMEM((width * size_y, width * size_y), BF),
            pltpu.SemaphoreType.DMA((2, size_x // CHUNK)),
            pltpu.SemaphoreType.DMA((3,)),
        ],
        compiler_params=PARAMS,
        cost_estimate=pl.CostEstimate(flops=int(4e9), bytes_accessed=1 << 22, transcendentals=0),
        name="relayout",
    )(occ, w1, w2, feat, cot)


def y_rims_kernel(one, two, to_a, to_b):
    size_x, size_y = one.shape[0] - 2, one.shape[1] - 2

    def lay(ref):
        def put(y):
            for which, src in enumerate((one, two)):
                ref[which] = src[1 : size_x + 1, y]

        return put

    by_parity(is_odd("depth"), 1, size_y, lay(to_a), lay(to_b))


def x_rims_kernel(one, two, after, to_a, to_b):
    def lay(ref):
        def put(x):
            for which, src in enumerate((one, two)):
                ref[which] = src[x]

        return put

    by_parity(is_odd("space"), 1, one.shape[0] - 2, lay(to_a), lay(to_b))


def rims(kernel, name, length, one, two, *after):
    shape = jax.ShapeDtypeStruct((2, length, *one.shape[2:]), BF)
    return pl.pallas_call(
        kernel,
        in_specs=[VM] * (2 + len(after)),
        out_specs=[VM, VM],
        out_shape=[shape, shape],
        compiler_params=PARAMS,
        cost_estimate=cost(0.1),
        name=name,
    )(one, two, *after)


def lay_y_kernel(one, two, da, db, after, one_out, two_out):
    size_x, size_y = one.shape[0] - 2, one.shape[1] - 2
    spot = jnp.where(is_odd("depth"), 0, size_y + 1)
    for which, dst in enumerate((one_out, two_out)):
        dst[1 : size_x + 1, pl.ds(spot, 1)] = da[which][:, None]
        dst[1 : size_x + 1, pl.ds(size_y + 1 - spot, 1)] = db[which][:, None]


def lay_x_kernel(one, two, sa, sb, after, one_out, two_out):
    size_x = one.shape[0] - 2
    spot = jnp.where(is_odd("space"), 0, size_x + 1)
    for which, dst in enumerate((one_out, two_out)):
        dst[pl.ds(spot, 1)] = sa[which][None]
        dst[pl.ds(size_x + 1 - spot, 1)] = sb[which][None]


def lay(kernel, name, one, two, got_a, got_b, after):
    shape = jax.ShapeDtypeStruct(one.shape, BF)
    return pl.pallas_call(
        kernel,
        in_specs=[VM] * 5,
        out_specs=[VM, VM],
        out_shape=[shape, shape],
        input_output_aliases={0: 0, 1: 1},
        compiler_params=PARAMS,
        cost_estimate=cost(0.1),
        name=name,
    )(one, two, got_a, got_b, after)


def block_input(padded, bx, pair):
    parts = []
    for by in pair:
        part = padded[pl.ds(BX * bx, IX), BY * by : BY * by + IY]
        parts.append(part.reshape(IX * IY * 32, 128))
    return jnp.concatenate(parts, 1)


def z_sum(product, half):
    n = BX * BY * 32
    p = product[:, half * 128 : (half + 1) * 128]
    lanes = lane_ids((n, 128))
    below = jnp.where(lanes > 0, pltpu.roll(p[:n], 1, 1), 0.0)
    above = jnp.where(lanes < 127, pltpu.roll(p[2 * n :], 127, 1), 0.0)
    return p[n : 2 * n] + below + above


def first_kernel(mask, t_one, t_two, p_in, p_og, *rest, edge, pairs):
    hid, pre = rest[-2:]
    last = (hid.shape[0] - 2) // BX - 1
    bxs = (0, last) if edge else range(1, last)
    for bx in bxs:
        x = pl.ds(1 + bx * BX, BX)
        for pair in pairs:
            one = jnp.dot(t_one[...], block_input(p_in, bx, pair), preferred_element_type=F32)
            two = jnp.dot(t_two[...], block_input(p_og, bx, pair), preferred_element_type=F32)
            for half, by in enumerate(pair):
                m = mask[bx * BX // BRICK, by * BY // BRICK]
                act = z_sum(one, half)
                grad = z_sum(two, half)
                sig = 1.0 / (1.0 + jnp.exp(-act))
                hidden = (act * sig * m).astype(BF)
                slope = (grad * sig * (1.0 + act * (1.0 - sig)) * m).astype(BF)
                y = slice(1 + by * BY, 1 + (by + 1) * BY)
                hid[x, y] = hidden.reshape(BX, BY, 32, 128)
                pre[x, y] = slope.reshape(BX, BY, 32, 128)


def first(mask, t_one, t_two, p_in, p_og, onto, edge, pairs):
    arr = jax.ShapeDtypeStruct(p_in.shape, BF)
    return pl.pallas_call(
        functools.partial(first_kernel, edge=edge, pairs=pairs),
        in_specs=[VM] * (5 + len(onto)),
        out_specs=[VM] * 2,
        out_shape=[arr] * 2,
        input_output_aliases={5: 0, 6: 1} if onto else {},
        compiler_params=PARAMS,
        cost_estimate=cost(5),
        name="first",
    )(mask, t_one, t_two, p_in, p_og, *onto)


def copies_out(held, out, bxs, sem):
    return [
        pltpu.make_async_copy(held.at[slot], out.at[pl.ds(bx * BX, BX)], sem.at[slot])
        for slot, bx in enumerate(bxs)
    ]


def second_kernel(mask, t, padded, after, *rest, bxs, prev_bxs, final, span, n_in):
    ins, rest = list(rest[:n_in]), list(rest[n_in:])
    copies = []
    if span:
        own, other = ins[:2]
        g_outs = [rest.pop(0), rest.pop(0)]
    if prev_bxs:
        out = rest.pop(0)
        prev, prev_sem = ins[2 if span else 0], rest.pop()
        copies += copies_out(prev, out, prev_bxs, prev_sem)
        for made in copies:
            made.start()
    if span:
        g_sem, wide = rest.pop(), rest.pop()
        finish_grads(own, other, wide, span)
        for k, ref in enumerate(g_outs):
            made = pltpu.make_async_copy(wide.at[k], ref, g_sem.at[k])
            made.start()
            copies.append(made)
    held = rest.pop(0)
    width, size_y = held.shape[2], held.shape[3]
    last_copies = copies_out(held, out, bxs, rest.pop()) if final else []
    shape = (BX * width * BY // 8, 8, 128)
    part = lax.broadcasted_iota(jnp.int32, shape, 1) // BY
    per = 8 // BY
    for slot, bx in enumerate(bxs):
        pairs = []
        for at in range(0, size_y // BY, per):
            m = mask[bx * BX // BRICK, at * BY // BRICK]
            blocks = []
            for pair in [(k, k + 1) for k in range(at, at + per, 2)]:
                product = jnp.dot(t[...], block_input(padded, bx, pair), preferred_element_type=F32)
                blocks += [(z_sum(product, h) * m).reshape(shape) for h in range(2)]
            columns = []
            for c in range(per):
                column = None
                for k in range(per):
                    turn = (k - c) * BY % 8
                    moved = pltpu.roll(blocks[k], turn, 1) if turn else blocks[k]
                    column = moved if k == 0 else jnp.where(part == k, moved, column)
                columns.append(column)
            pairs.append(jnp.stack(columns, 1).reshape(BX, width, 8, 128))
        held[slot] = jnp.concatenate(pairs, 2).astype(BF)
        if final:
            last_copies[slot].start()
    for made in copies + last_copies:
        made.wait()


def second(mask, t, padded, after, bxs, prev=None, grads=(), span=0, final=False, us=4):
    size_x, size_y, width, size_z = padded.shape
    size_x, size_y = size_x - 2, size_y - 2
    held = (len(bxs), BX, width, size_y, size_z)
    prev_held, prev_bxs, onto = prev or (None, (), None)
    extra = list(grads) + ([prev_held] if prev else []) + ([] if onto is None else [onto])
    outs = [jax.ShapeDtypeStruct((32, 27 * 32), F32)] * len(grads)
    if prev:
        outs.append(jax.ShapeDtypeStruct((size_x, width, size_y, size_z), BF))
    specs = [HB] * len(outs)
    scratch = []
    if final:
        scratch.append(VMEM(held, BF))
        scratch.append(pltpu.SemaphoreType.DMA((len(bxs),)))
    else:
        outs.append(jax.ShapeDtypeStruct(held, BF))
        specs.append(VM)
    if grads:
        scratch += [VMEM((2, 32, 27 * 32), F32), pltpu.SemaphoreType.DMA((2,))]
    if prev:
        scratch.append(pltpu.SemaphoreType.DMA((len(prev_bxs),)))
    n_in = len(extra)
    in_specs = [VM] * (4 + n_in - (onto is not None)) + [HB] * (onto is not None)
    return pl.pallas_call(
        functools.partial(
            second_kernel, bxs=bxs, prev_bxs=prev_bxs, final=final, span=span, n_in=n_in
        ),
        in_specs=in_specs,
        out_specs=specs,
        out_shape=outs,
        input_output_aliases={} if onto is None else {3 + n_in: len(grads)},
        scratch_shapes=scratch,
        compiler_params=PARAMS,
        cost_estimate=cost(us),
        name="second",
    )(mask, t, padded, after, *extra)


def grad_sum(g, padded, total):
    size_y = g.shape[1] - 2
    n = BX * BY * 32
    lhs, rhs = [], []
    for bx in range((g.shape[0] - 2) // BX):
        for by in range(size_y // BY):
            x, y = pl.ds(1 + bx * BX, BX), slice(1 + by * BY, 1 + (by + 1) * BY)
            block = g[x, y].reshape(n, 128).astype(F32)
            lanes = lane_ids((n, 128))
            ahead = jnp.where(lanes < 127, pltpu.roll(block, 127, 1), 0.0)
            behind = jnp.where(lanes > 0, pltpu.roll(block, 1, 1), 0.0)
            lhs.append(jnp.concatenate([ahead, block, behind], 0).astype(BF))
        rhs += [block_input(padded, bx, (at, at + 1)) for at in range(0, size_y // BY, 2)]
    lhs, rhs = jnp.concatenate(lhs, 1), jnp.concatenate(rhs, 1)
    total[...] = lax.dot_general(lhs, rhs, (((1,), (1,)), ((), ())), preferred_element_type=F32)


def grad_taps(total, out):
    lanes = IX * IY * 32
    for dz in range(3):
        acc = jnp.zeros((32, lanes), F32)
        for xo in range(BX):
            for yo in range(BY):
                row = ((dz * BX + xo) * BY + yo) * 32
                part = total[row : row + 32, :]
                shift = (xo * IY + yo) * 32
                acc += pltpu.roll(part, lanes - shift, 1) if shift else part
        for dx in range(3):
            at = dx * IY * 32
            moved = pltpu.roll(acc, lanes - at, 1) if at else acc
            out[dx, dz * 32 : (dz + 1) * 32, :] = moved[:, :128]


def grad_one_kernel(g, padded, out, total):
    grad_sum(g, padded, total)
    grad_taps(total, out)


def grad_two_kernel(g, padded, one, after, keep, send, taps, total):
    grad_sum(g, padded, total)
    grad_taps(total, taps)

    def store(ref):
        def put(value):
            ref[...] = value

        return put

    by_parity(is_odd("depth"), taps[...], one[...], store(keep), store(send))


def kernel_grad(kernel, g, padded, extra=(), outs=1, scratch=()):
    taps = jax.ShapeDtypeStruct((3, 96, 128), F32)
    return pl.pallas_call(
        kernel,
        in_specs=[VM] * (2 + len(extra)),
        out_specs=[VM] * outs,
        out_shape=[taps] * outs,
        scratch_shapes=list(scratch) + [VMEM((3 * BX * BY * 32, IX * IY * 32), F32)],
        compiler_params=PARAMS,
        cost_estimate=cost(8),
        name="kernel_grad",
    )(g, padded, *extra)


def finish_grads(own, other, wide, span):
    def zeros():
        return [jnp.zeros((32, 128), F32) for _ in range(7)]

    def write(acc, out):
        for k in range(7):
            end = min((k + 1) * 128, wide.shape[2])
            wide[out, :, k * 128 : end] = acc[k][:, : end - k * 128] / span

    def both(one, two):
        acc = zeros()
        for dx in range(3):
            for dz in range(3):
                block = one[dx, dz * 32 : (dz + 1) * 32, :]
                for dy in range(3):
                    place(acc, block, dy * 32, ((dx * 3 + dy) * 3 + dz) * 32)
        write(acc, 0)
        acc = zeros()
        pad = jnp.zeros((96, 128), F32)
        for dx in range(3):
            for dz in range(3):
                block = two[dx, dz * 32 : (dz + 1) * 32, :]
                turned = jnp.concatenate([block, pad], 0).T
                for dy in range(3):
                    tap = ((2 - dx) * 3 + 2 - dy) * 3 + 2 - dz
                    place(acc, turned[dy * 32 : (dy + 1) * 32], 0, tap * 32)
        write(acc, 1)

    odd = is_odd("depth")

    @pl.when(odd)
    def _():
        both(other, own)

    @pl.when(jnp.logical_not(odd))
    def _():
        both(own, other)


def swap(x, axis, phase):
    n = lax.axis_size(axis)
    pairs = []
    for i in range(phase, n - 1, 2):
        pairs += [(i, i + 1), (i + 1, i)]
    return lax.ppermute(x, axis, pairs)


def both_phases(to_a, to_b, axis):
    return swap(to_a, axis, 0), swap(to_b, axis, 1)


def add_kernel(x, y, after, out):
    out[...] = (x[...].astype(F32) + y[...].astype(F32)).astype(out.dtype)


def add_after(x, y, after, dtype=F32):
    return pl.pallas_call(
        add_kernel,
        in_specs=[VM, VM, VM],
        out_specs=VM,
        out_shape=jax.ShapeDtypeStruct(x.shape, dtype),
        compiler_params=PARAMS,
        cost_estimate=cost(0.1),
        name="add_after",
    )(x, y, after)


def partner(x, axis, step):
    return lax.ppermute(x, axis, [(i, i ^ step) for i in range(lax.axis_size(axis))])


def shards(features, occupancy, weight_one, weight_two, cotangent):
    span = features.shape[0] * lax.axis_size("space")

    size_x, size_y = features.shape[0], features.shape[2]
    by = range(size_y // BY)
    middle, ends = [by[k : k + 2] for k in by[1:-1:2]], [(by[0], by[-1])]

    args = (occupancy, weight_one, weight_two, features, cotangent)
    in_hbm = [pltpu.with_memory_space_constraint(v, pltpu.HBM) for v in args]
    mask, t1, t2b, t2, t1b, p_in, p_og = relayout(*in_hbm)
    da, db = both_phases(*rims(y_rims_kernel, "y_rims", size_x, p_in, p_og), "depth")
    out = first(mask, t1, t2b, p_in, p_og, (), False, middle)
    p_in, p_og = lay(lay_y_kernel, "lay_y", p_in, p_og, da, db, out[0])
    to_a, to_b = rims(x_rims_kernel, "x_rims", size_y + 2, p_in, p_og, t2)
    sa, sb = both_phases(to_a, to_b, "space")
    out = first(mask, t1, t2b, p_in, p_og, out, False, ends)
    p_in, p_og = lay(lay_x_kernel, "lay_x", p_in, p_og, sa, sb, out[0])
    hid, pre = first(mask, t1, t2b, p_in, p_og, out, True, middle + ends)

    da, db = both_phases(*rims(y_rims_kernel, "y_rims", size_x, hid, pre), "depth")
    (g_one,) = kernel_grad(grad_one_kernel, pre, p_in)
    hid, pre = lay(lay_y_kernel, "lay_y", hid, pre, da, db, g_one)
    to_a, to_b = rims(x_rims_kernel, "x_rims", size_y + 2, hid, pre, g_one)
    sa, sb = both_phases(to_a, to_b, "space")
    taps = VMEM((3, 96, 128), F32)
    keep, send = kernel_grad(grad_two_kernel, hid, p_og, (g_one, to_a), 2, [taps])
    steps = [("depth", 1 << k) for k in range(1, lax.axis_size("depth").bit_length() - 1)]
    steps += [("space", 1 << k) for k in range(lax.axis_size("space").bit_length() - 1)]
    types = [BF] * 3 + [F32] * (len(steps) - 2)
    total = add_after(keep, swap(send, "depth", 0), keep, types[0])
    n = size_x // BX
    inner, low, high = tuple(range(2, n - 2)), (0, 1), (n - 2, n - 1)
    received = partner(total, *steps[0])
    (held_a,) = second(mask, t2, hid, total, inner)
    total = add_after(total, received, held_a, types[1])
    received = partner(total, *steps[1])
    output, held_b = second(mask, t1b, pre, total, inner, (held_a, inner, None))
    total = add_after(total, received, held_b, types[2])
    hid, pre = lay(lay_x_kernel, "lay_x", hid, pre, sa, sb, held_b)
    received = partner(total, *steps[2])
    edges = low + high
    grad_input, held_c = second(mask, t2, hid, total, edges, (held_b, inner, None))
    output, held_d = second(mask, t1b, pre, held_c, low, (held_c, edges, output), us=2)
    total = add_after(total, received, held_d, types[3])
    for step, kind in zip(steps[3:], types[4:]):
        total = add_after(total, partner(total, *step), held_d, kind)
    other = swap(total, "depth", 0)
    grad_one, grad_two, grad_input = second(
        mask, t1b, pre, held_d, high, (held_d, low, grad_input), (total, other), span, True, us=3
    )
    return output, grad_input, grad_one, grad_two


def solution(mesh):
    field = P(("groups", "space"), None, "depth", None)
    in_specs = (field, P(("groups", "space"), "depth", None), P(), P(), field)
    out_specs = (field, field, P("groups", None), P("groups", None))
    return jax.shard_map(shards, mesh=mesh, in_specs=in_specs, out_specs=out_specs, check_vma=False)
```
